256 devices in a mesh: subset: 16 (over x, z_lo, core), slab: 16 (over y, z_hi).
Axes of the slice: x: 4, y: 4, z: 8 (z_hi: 4, z_lo: 2; z = z_hi * 2 + z_lo), core: 2. Of those that a mesh axis runs over, the one named last changes fastest.
Arguments:
- sinogram: bfloat16 [512, 128, 2048], P(('subset', 'slab')), may hold values from -12 to 12
- angles: float32 [512], P(('subset', 'slab')), may hold values from -3.140625 to 3.140625
- w_first: float32 [32, 27], replicated, may hold values from -1.25 to 1.25
- b_first: float32 [32], replicated, may hold values from -3 to 3
- w_second: float32 [32, 27], replicated, may hold values from -0.21875 to 0.21875
- b_second: float32 [1], replicated, may hold values from -3 to 3
Outputs:
- prediction: float32 [16, 64, 8, 1024], P('subset', 'slab')
- target_slab: float32 [16, 64, 8, 1024], P('subset', 'slab')
- loss: float32 [], replicated
- grad_w_first: float32 [32, 27], replicated
- grad_b_first: float32 [32], replicated
- grad_w_second: float32 [32, 27], replicated
- grad_b_second: float32 [1], replicated
The draws below stay inside these ranges and needn't reach their ends.
All inputs are finite; a program needn't handle non-finite values.
Results may differ from the reference program's by a relative error of at most 0.00065.
The reference program's roundings to bfloat16 on the way (of `weights`) count: a program that leaves them out, or rounds other values in their place, can miss the bound.
Values may be sent and summed in bfloat16 or wider, within the bound.
A program may use at most 128 MiB of HBM per device.

```python
import math
import jax
import jax.numpy as jnp
from jax import lax

DET = 2048
CH = 32
X = 1024
Y = 8
Z = 128
SUBSETS = 8
VPS = 64
VIEWS = 512


def draw_sinogram(key, part):
    key_base = jax.random.fold_in(key, 11)
    view_scale = jnp.exp(jnp.log(3.0) * (jnp.arange(VIEWS, dtype=jnp.float32) / max(VIEWS - 1, 1) - 0.5))
    slice_scale = jnp.exp(jnp.log(3.0) * (jnp.arange(Z, dtype=jnp.float32) / max(Z - 1, 1) - 0.5))
    scales = view_scale[:, None, None] * slice_scale[None, :, None]
    base = jax.random.normal(key_base, (VIEWS, Z, DET), jnp.float32)
    values = base * scales
    return jnp.clip(values, -12.0, 12.0).astype(jnp.bfloat16)


def normal_values(stream_key, extent, spread, bound, held_as=jnp.bfloat16):
    values = jax.random.normal(stream_key, extent, jnp.float32) * spread
    return jnp.minimum(jnp.maximum(values, -bound), bound).astype(held_as)


def setup_inputs(seed: int = 0) -> dict:
    seeds = jax.random.split(jax.random.key(seed), 7)
    sinogram = draw_sinogram(jax.random.fold_in(seeds[6], 71), 0)
    angles = jnp.clip(jax.random.uniform(seeds[1], (VIEWS,), jnp.float32, -3.140625, 3.140625), -3.140625, 3.140625)
    w_first = normal_values(seeds[2], (CH, 27), 27 ** -0.5, 1.25, jnp.float32)
    b_first = normal_values(seeds[3], (CH,), 0.5, 3.0, jnp.float32)
    w_second = normal_values(seeds[4], (CH, 27), (27 * CH) ** -0.5, 0.21875, jnp.float32)
    b_second = normal_values(seeds[5], (1,), 0.5, 3.0, jnp.float32)
    return dict(sinogram=sinogram, angles=angles, w_first=w_first, b_first=b_first, w_second=w_second, b_second=b_second)


def make_patches(field_pad, depth):
    rows = field_pad.shape[1]
    cols = field_pad.shape[2]
    padded = jnp.pad(field_pad, ((0, 0), (1, 1), (1, 1)))
    pieces = []
    for shift_z in range(3):
        for shift_y in range(3):
            for shift_x in range(3):
                pieces.append(padded[shift_z:shift_z + depth, shift_y:shift_y + rows, shift_x:shift_x + cols].reshape(-1))
    return jnp.stack(pieces)

def conv_second(hidden_pad, w_second, depth, rows, cols):
    channels = hidden_pad.shape[0]
    taps = jnp.dot(w_second.T, hidden_pad.reshape(channels, -1), precision=lax.Precision.HIGHEST)
    taps = taps.reshape(27, depth + 2, rows + 2, cols + 2)
    added = jnp.zeros((depth, rows, cols), jnp.float32)
    for shift_z in range(3):
        for shift_y in range(3):
            for shift_x in range(3):
                added = added + taps[9 * shift_z + 3 * shift_y + shift_x, shift_z:shift_z + depth, shift_y:shift_y + rows, shift_x:shift_x + cols]
    return added

def network(params, inp):
    w_first, b_first, w_second, b_second = params
    channels = w_first.shape[0]
    inp_pad = jnp.pad(inp, ((1, 1), (0, 0), (0, 0)))
    patches = make_patches(inp_pad, Z)
    pre_act = jnp.dot(w_first, patches, precision=lax.Precision.HIGHEST) + b_first[:, None]
    hidden = jax.nn.relu(pre_act).reshape(channels, Z, Y, X)
    hidden_pad = jnp.pad(hidden, ((0, 0), (1, 1), (1, 1), (1, 1)))
    added = conv_second(hidden_pad, w_second, Z, Y, X)
    return inp + added + b_second[0]

def reference(sinogram, angles, w_first, b_first, w_second, b_second):
    subsets = SUBSETS
    group_views = VPS
    sino = sinogram.reshape(subsets, group_views, Z, DET)
    angle_rows = angles.reshape(subsets, group_views)
    columns = jnp.arange(X, dtype=jnp.float32) - (X - 1) / 2.0
    row_pos = jnp.arange(Y, dtype=jnp.float32) - (Y - 1) / 2.0

    def one_view(running, item):
        block_sino, block_angle = item
        positions = columns[None, None, :] * jnp.cos(block_angle)[:, None, None] + row_pos[None, :, None] * jnp.sin(block_angle)[:, None, None] + (DET - 1) / 2.0
        positions = positions.reshape(subsets, -1)
        lower = jnp.floor(positions)
        weight_low = jnp.maximum(0.0, 1.0 - jnp.abs(positions - lower)).astype(jnp.bfloat16)
        weight_high = jnp.maximum(0.0, 1.0 - jnp.abs(positions - (lower + 1.0))).astype(jnp.bfloat16)
        lower_index = jnp.clip(lower.astype(jnp.int32), 0, DET - 2)
        val_low = jnp.take_along_axis(block_sino, lower_index[:, None, :], axis=2)
        val_high = jnp.take_along_axis(block_sino, (lower_index + 1)[:, None, :], axis=2)
        contrib = weight_low[:, None, :].astype(jnp.float32) * val_low.astype(jnp.float32) + weight_high[:, None, :].astype(jnp.float32) * val_high.astype(jnp.float32)
        return (running + contrib, None)
    start = jnp.zeros((subsets, Z, Y * X), jnp.float32)
    summed, _ = lax.scan(one_view, start, (jnp.swapaxes(sino, 0, 1), angle_rows.T))
    recon = summed.reshape(subsets, Z, Y, X) * (math.pi / group_views)
    total = lax.optimization_barrier(jnp.sum(recon, axis=0))
    target = (total[None] - recon) / (subsets - 1)
    cells_all = float(subsets * Z * Y * X)
    params = (w_first, b_first, w_second, b_second)

    def per_subset(item):
        inp, tgt = item

        def loss_fn(weights):
            pred = network(weights, inp)
            return (jnp.sum((pred - tgt) ** 2) / cells_all, pred)
        value, grad_fn, pred = jax.vjp(loss_fn, params, has_aux=True)
        grads = grad_fn(jnp.float32(1.0))[0]
        return (pred, value, grads)
    preds, losses, grads = lax.map(per_subset, (recon, target))
    grads = jax.tree.map(lambda part: lax.optimization_barrier(jnp.sum(part, axis=0)), grads)
    preds_out = preds.reshape(subsets * 2, Z // 2, Y, X)
    target_out = target.reshape(subsets * 2, Z // 2, Y, X)
    return (preds_out, target_out, jnp.sum(losses), grads[0], grads[1], grads[2], grads[3])
```

```python
import math

import jax
import jax.numpy as jnp
from jax import lax
from jax.experimental import pallas as pl
from jax.experimental.pallas import tpu as pltpu
from jax.sharding import Mesh
from jax.sharding import PartitionSpec as P

DET = 2048
X = 1024
Y = 8
DEPTH = 4
SUBS = 8
SLABS = 16
GROUP = 2 * SLABS
VPS = 64
FIRST_COL = 384
COLS = 1280
PATCH = 80
CELLS = float(SUBS * 128 * Y * X)
MESH = pl.DeviceIdType.MESH
F32 = jnp.float32
BF16 = jnp.bfloat16

GATHER = lax.GatherDimensionNumbers(
    offset_dims=(),
    collapsed_slice_dims=(1,),
    start_index_map=(1,),
    operand_batching_dims=(0,),
    start_indices_batching_dims=(0,),
)


def iota(shape, dim):
    return lax.broadcasted_iota(jnp.int32, shape, dim)


def exact_dot(a, b):
    return jnp.dot(a, b, precision=lax.Precision.HIGHEST, preferred_element_type=F32)


def dot_nt(a, b, precision=None):
    return lax.dot_general(
        a, b, (((1,), (1,)), ((), ())), precision=precision, preferred_element_type=F32
    )


def split(value):
    high = value.astype(BF16)
    return high, (value - high.astype(F32)).astype(BF16)


def tap_of(column, shift_y):
    block = column >> 3
    shift_z = (block >= 3).astype(jnp.int32) + (block >= 6).astype(jnp.int32)
    return 6 * shift_z + block + 3 * shift_y


def build_first(w_first, b_first):
    pick = (iota((256, 32), 0) >> 3 == iota((256, 32), 1)).astype(F32)
    rows = exact_dot(pick, w_first)
    bias = jnp.sum(pick * b_first, axis=1, keepdims=True)
    row, col = iota((256, PATCH), 0), iota((256, PATCH), 1)
    out = jnp.where(col == 72, bias, 0.0)
    for shift_y in range(3):
        expand = iota((27, PATCH), 0) == tap_of(iota((27, PATCH), 1), shift_y)
        expand = (expand & (iota((27, PATCH), 1) < 72)).astype(F32)
        near = (col & 7) - (row & 7) == shift_y - 1
        out = out + jnp.where(near & (col < 72), exact_dot(rows, expand), 0.0)
    high, low = split(out)
    return jnp.concatenate([high, low, high], axis=1)


def build_second(w_second):
    pick = (iota((256, 32), 0) >> 3 == iota((256, 32), 1)).astype(F32)
    rows = exact_dot(pick, w_second)
    row, col = iota((256, PATCH), 0), iota((256, PATCH), 1)
    pick_t = (iota((32, 256), 1) >> 3 == iota((32, 256), 0)).astype(F32)
    row_t, col_t = iota((PATCH, 256), 0), iota((PATCH, 256), 1)
    out = jnp.zeros((256, PATCH), F32)
    out_t = jnp.zeros((PATCH, 256), F32)
    for shift_y in range(3):
        expand = iota((27, PATCH), 0) == tap_of(iota((27, PATCH), 1), shift_y)
        expand = (expand & (iota((27, PATCH), 1) < 72)).astype(F32)
        near = (row & 7) - (col & 7) == shift_y - 1
        out = out + jnp.where(near & (col < 72), exact_dot(rows, expand), 0.0)
        expand_t = iota((PATCH, 27), 1) == tap_of(iota((PATCH, 27), 0), shift_y)
        expand_t = (expand_t & (iota((PATCH, 27), 0) < 72)).astype(F32)
        taps_t = dot_nt(expand_t, w_second, lax.Precision.HIGHEST)
        near_t = (col_t & 7) - (row_t & 7) == shift_y - 1
        out_t = out_t + jnp.where(near_t & (row_t < 72), exact_dot(taps_t, pick_t), 0.0)
    high, low = split(out)
    return jnp.concatenate([high, low, high], axis=1), jnp.concatenate(split(out_t), axis=0)


def gather_grads(first, second):
    pick_t = (iota((32, 256), 1) >> 3 == iota((32, 256), 0)).astype(F32)
    row, col = iota((256, PATCH), 0), iota((256, PATCH), 1)
    frow, fcol = iota((PATCH, 128), 0), iota((PATCH, 128), 1)
    out = jnp.zeros((32, 128), F32)
    for shift_y in range(3):
        near = ((col & 7) - (row & 7) == shift_y - 1) & (col < 72)
        to = (fcol == tap_of(frow, shift_y)) & (frow < 72)
        if shift_y == 1:
            near = near | (col == 72)
            to = to | ((frow == 72) & (fcol == 27))
        out = out + exact_dot(exact_dot(pick_t, jnp.where(near, first, 0.0)), to.astype(F32))
        near = ((row & 7) - (col & 7) == shift_y - 1) & (col < 72)
        to = (fcol == tap_of(frow, shift_y) + 32) & (frow < 72)
        out = out + exact_dot(exact_dot(pick_t, jnp.where(near, second, 0.0)), to.astype(F32))
    return out


def shifted(value, by):
    lane = iota(value.shape, 1)
    if by == 1:
        return jnp.where(lane == 0, 0.0, pltpu.roll(value, 1, 1))
    return jnp.where(lane == X - 1, 0.0, pltpu.roll(value, X - 1, 1))


def exchange_kernel(
    sino,
    table,
    w_first,
    b_first,
    w_second,
    recv,
    tables,
    first_cat,
    second_cat,
    second_t,
    send,
    send_sem,
    recv_sem,
    tsend_sem,
    trecv_sem,
):
    sub, half, slab = lax.axis_index("sub"), lax.axis_index("half"), lax.axis_index("slab")
    me = half * SLABS + slab

    def peer(other):
        return (sub, other // SLABS, lax.rem(other, SLABS))

    def signal(p, carry):
        other = lax.rem(me + p, GROUP)
        pl.semaphore_signal(
            pltpu.get_barrier_semaphore(), inc=1, device_id=peer(other), device_id_type=MESH
        )
        return carry

    lax.fori_loop(1, GROUP, signal, 0)

    def pack(q, carry):
        at = pl.multiple_of(q * 16, 16)
        zero = sino[0, pl.ds(at, 16), FIRST_COL : FIRST_COL + COLS].astype(F32)
        one = sino[1, pl.ds(at, 16), FIRST_COL : FIRST_COL + COLS].astype(F32)
        for i in range(4):
            rows = jnp.concatenate([zero[4 * i : 4 * i + 4], one[4 * i : 4 * i + 4]], axis=0)
            send[4 * q + i] = jnp.concatenate(
                [rows[:, : COLS // 2], rows[:, COLS // 2 :]], axis=0
            ).astype(BF16)
        return carry

    lax.fori_loop(0, GROUP // 4, pack, 0)
    recv[me] = send[me]
    tables[me] = table[...]
    pl.semaphore_wait(pltpu.get_barrier_semaphore(), GROUP - 1)

    def copies(p):
        other = lax.rem(me + p, GROUP)
        data = pltpu.make_async_remote_copy(
            src_ref=send.at[other],
            dst_ref=recv.at[me],
            send_sem=send_sem.at[other],
            recv_sem=recv_sem.at[me],
            device_id=peer(other),
            device_id_type=MESH,
        )
        small = pltpu.make_async_remote_copy(
            src_ref=table,
            dst_ref=tables.at[me],
            send_sem=tsend_sem.at[other],
            recv_sem=trecv_sem.at[me],
            device_id=peer(other),
            device_id_type=MESH,
        )
        return data, small

    def arrivals(p):
        other = lax.rem(me + p, GROUP)
        data = pltpu.make_async_remote_copy(
            src_ref=send.at[other],
            dst_ref=recv.at[other],
            send_sem=send_sem.at[other],
            recv_sem=recv_sem.at[other],
            device_id=peer(other),
            device_id_type=MESH,
        )
        small = pltpu.make_async_remote_copy(
            src_ref=table,
            dst_ref=tables.at[other],
            send_sem=tsend_sem.at[other],
            recv_sem=trecv_sem.at[other],
            device_id=peer(other),
            device_id_type=MESH,
        )
        return data, small

    def start(p, carry):
        for copy in copies(p):
            copy.start()
        return carry

    lax.fori_loop(1, GROUP, start, 0)
    first_cat[...] = build_first(w_first[...], b_first[...])
    second_cat[...], second_t[...] = build_second(w_second[...])

    def finish(p, carry):
        for copy in arrivals(p):
            copy.wait()
        return carry

    lax.fori_loop(1, GROUP, finish, 0)


def take(source, index):
    return lax.gather(
        source, index[..., None], GATHER, (1, 1), mode=lax.GatherScatterMode.PROMISE_IN_BOUNDS
    )


def backproject_kernel(table, recv, out, rows):
    def widen(s, carry):
        block = recv[s].astype(F32)
        row = jnp.concatenate([block[:8], block[8:]], axis=1)
        rows[0, s] = row
        rows[1, s] = pltpu.roll(row, COLS - 64, 1)
        return carry

    lax.fori_loop(0, GROUP, widen, 0)
    row_pos = iota((8, 128), 0).astype(F32) - (Y - 1) / 2.0
    lane = iota((8, 128), 1).astype(F32)
    out[...] = jnp.zeros_like(out)

    def one_sender(s, carry):
        for block in range(X // 128):
            here = slice(block * 128, (block + 1) * 128)
            total = [out[z, :, here] for z in range(DEPTH)]
            for v in range(2):
                cosine, sine = table[s, 2 * v], table[s, 2 * v + 1]
                step = table[s, 4 + v * 8 + block].astype(jnp.int32)
                pos = (
                    (lane + (128.0 * block - (X - 1) / 2.0)) * cosine + row_pos * sine
                ) + (DET - 1) / 2.0
                lower = jnp.floor(pos)
                part = pos - lower
                w_high = part.astype(BF16).astype(F32)
                w_low = (1.0 - part).astype(BF16).astype(F32)
                index = lower.astype(jnp.int32) - (FIRST_COL + 64 * step)
                index = jnp.concatenate([index, index], axis=0)
                at_low = (index & 127).astype(jnp.int16)
                at_high = ((index + 1) & 127).astype(jnp.int16)
                whole = index.astype(jnp.int16)
                in_low = whole < jnp.int16(128)
                in_high = whole < jnp.int16(127)
                copy = step & 1
                at = pl.multiple_of((step >> 1) * 128, 128)
                for pair in range(2):

                    def source(offset):
                        parts = [
                            jnp.broadcast_to(
                                rows[
                                    copy, s, pl.ds(v * 4 + 2 * pair + q, 1), pl.ds(at + offset, 128)
                                ],
                                (8, 128),
                            )
                            for q in range(2)
                        ]
                        return jnp.concatenate(parts, axis=0).astype(BF16)

                    near, far = source(0), source(128)
                    low = jnp.where(in_low, take(near, at_low), take(far, at_low)).astype(F32)
                    high = jnp.where(in_high, take(near, at_high), take(far, at_high)).astype(F32)
                    for q in range(2):
                        z = 2 * pair + q
                        half = slice(8 * q, 8 * q + 8)
                        total[z] = total[z] + (w_low * low[half] + w_high * high[half])
            for z in range(DEPTH):
                out[z, :, here] = total[z]
        return carry

    lax.fori_loop(0, GROUP, one_sender, 0)
    out[...] = out[...] * (math.pi / VPS)


def network_kernel(
    own,
    first_cat,
    second_cat,
    second_t,
    b_second,
    pred_out,
    target_out,
    grads_out,
    field,
    totals,
    near_u,
    patch_u,
    hidden_all,
    taps,
    near_r,
    acc_first,
    acc_second,
    part_slots,
    whole_slots,
    mine,
    halo_send,
    halo_recv,
    tot_send,
    tot_recv,
    slab_send,
    slab_recv,
    sub_send,
    sub_recv,
):
    sub, half, slab = lax.axis_index("sub"), lax.axis_index("half"), lax.axis_index("slab")
    me = half * SLABS + slab
    pair = sub * 2 + half

    def ring(other):
        return (sub, other // SLABS, lax.rem(other, SLABS))

    before = ring(lax.rem(me + GROUP - 1, GROUP))
    after = ring(lax.rem(me + 1, GROUP))

    def slab_peer(p):
        other = lax.rem(slab + p, SLABS)
        return other, (sub, half, other)

    def pair_peer(p):
        other = lax.rem(pair + p, 2 * SUBS)
        return other, (other // 2, lax.rem(other, 2), slab)

    def sub_peer(p):
        other = lax.rem(sub + p, SUBS)
        return other, (other, half, slab)

    barrier = pltpu.get_barrier_semaphore()
    for target in (before, after):
        pl.semaphore_signal(barrier, inc=1, device_id=target, device_id_type=MESH)

    def greet(p, carry):
        for peer in (slab_peer, pair_peer):
            pl.semaphore_signal(
                pltpu.get_barrier_semaphore(), inc=1, device_id=peer(p)[1], device_id_type=MESH
            )
        return carry

    lax.fori_loop(1, 16, greet, 0)
    pl.semaphore_wait(barrier, 32)

    to_after = pltpu.make_async_remote_copy(
        src_ref=own.at[2:4],
        dst_ref=field.at[0:2],
        send_sem=halo_send.at[0],
        recv_sem=halo_recv.at[0],
        device_id=after,
        device_id_type=MESH,
    )
    to_before = pltpu.make_async_remote_copy(
        src_ref=own.at[0:2],
        dst_ref=field.at[6:8],
        send_sem=halo_send.at[1],
        recv_sem=halo_recv.at[1],
        device_id=before,
        device_id_type=MESH,
    )
    to_after.start()
    to_before.start()

    def total_copy(p, slot):
        other, target = sub_peer(p)
        return pltpu.make_async_remote_copy(
            src_ref=own,
            dst_ref=totals.at[sub if slot is None else other],
            send_sem=tot_send.at[other],
            recv_sem=tot_recv.at[sub if slot is None else other],
            device_id=target,
            device_id_type=MESH,
        )

    def send_total(p, carry):
        total_copy(p, None).start()
        return carry

    lax.fori_loop(1, SUBS, send_total, 0)
    field[2:6] = own[...]
    totals[sub] = own[...]
    taps[...] = jnp.zeros_like(taps)
    near_r[...] = jnp.zeros_like(near_r)
    acc_first[...] = jnp.zeros_like(acc_first)
    acc_second[...] = jnp.zeros_like(acc_second)
    to_after.wait()
    to_before.wait()

    for m in range(8):
        value = field[m]
        if m < 2:
            value = jnp.where(me > 0, value, 0.0)
        if m >= 6:
            value = jnp.where(me < GROUP - 1, value, 0.0)
        near_u[m] = jnp.concatenate([shifted(value, 1), value, shifted(value, -1)], axis=0)

    ones = (iota((8, X), 0) == 0).astype(F32)

    def forward(j, carry):
        patch = jnp.concatenate([near_u[j], near_u[j + 1], near_u[j + 2], ones], axis=0)
        high, low = split(patch)
        patch_u[j] = high
        pre = jnp.dot(
            first_cat[...], jnp.concatenate([high, high, low], axis=0), preferred_element_type=F32
        )
        outside = ((j == 0) & (me == 0)) | ((j == 5) & (me == GROUP - 1))
        hidden = jnp.maximum(pre, 0.0) * jnp.where(outside, 0.0, 1.0)
        high, low = split(hidden)
        hidden_all[j] = high
        main = jnp.dot(second_t[...], high, preferred_element_type=F32)
        rest = jnp.dot(second_t[0:PATCH], low, preferred_element_type=F32)
        added = main[:72] + (main[PATCH : PATCH + 72] + rest[:72])
        for shift_z in range(3):
            at = j - shift_z + 2
            taps[at] = taps[at] + added[24 * shift_z : 24 * shift_z + 24]
        return carry

    lax.fori_loop(0, 6, forward, 0)

    def finish_total(p, carry):
        total_copy(p, 1).wait()
        return carry

    lax.fori_loop(1, SUBS, finish_total, 0)

    sum_square = jnp.zeros((8, X), F32)
    sum_resid = jnp.zeros((8, X), F32)
    for i in range(DEPTH):
        value = own[i]
        conv = shifted(taps[i + 2, 0:8], 1) + taps[i + 2, 8:16] + shifted(taps[i + 2, 16:24], -1)
        pred = value + conv + b_second[0]
        total = totals[0, i]
        for s in range(1, SUBS):
            total = total + totals[s, i]
        target = (total - value) / (SUBS - 1)
        pred_out[i] = pred
        target_out[i] = target
        diff = pred - target
        resid = (2.0 * diff) / CELLS
        sum_square = sum_square + diff * diff
        sum_resid = sum_resid + resid
        near_r[i + 2] = jnp.concatenate([shifted(resid, -1), resid, shifted(resid, 1)], axis=0)

    nothing = jnp.zeros((8, X), F32)

    def backward(j, carry):
        patch = jnp.concatenate([near_r[j + 2], near_r[j + 1], near_r[j], nothing], axis=0)
        high, low = split(patch)
        grad = jnp.dot(
            second_cat[...], jnp.concatenate([high, high, low], axis=0), preferred_element_type=F32
        )
        hidden = hidden_all[j]
        acc_second[...] += dot_nt(hidden, high)
        grad = jnp.where(hidden.astype(F32) > 0.0, grad, 0.0).astype(BF16)
        acc_first[...] += dot_nt(grad, patch_u[j])
        return carry

    lax.fori_loop(0, 6, backward, 0)

    packed = gather_grads(acc_first[...], acc_second[...])
    row, lane = iota((32, 128), 0), iota((32, 128), 1)
    packed = packed + jnp.where(
        (row == 0) & (lane == 64), jnp.sum(sum_square) / CELLS, 0.0
    )
    packed = packed + jnp.where((row == 0) & (lane == 65), jnp.sum(sum_resid), 0.0)

    mine[0] = packed
    part_slots[slab] = packed

    def slab_copy(p, arriving):
        other, target = slab_peer(p)
        slot = other if arriving else slab
        return pltpu.make_async_remote_copy(
            src_ref=mine.at[0],
            dst_ref=part_slots.at[slot],
            send_sem=slab_send.at[other],
            recv_sem=slab_recv.at[slot],
            device_id=target,
            device_id_type=MESH,
        )

    def pair_copy(p, arriving):
        other, target = pair_peer(p)
        slot = other if arriving else pair
        return pltpu.make_async_remote_copy(
            src_ref=mine.at[1],
            dst_ref=whole_slots.at[slot],
            send_sem=sub_send.at[other],
            recv_sem=sub_recv.at[slot],
            device_id=target,
            device_id_type=MESH,
        )

    def started(make):
        def step(p, carry):
            make(p, False).start()
            return carry

        lax.fori_loop(1, 16, step, 0)

    def finished(make):
        def step(p, carry):
            make(p, True).wait()
            return carry

        lax.fori_loop(1, 16, step, 0)

    started(slab_copy)
    finished(slab_copy)
    packed = part_slots[0]
    for s in range(1, 16):
        packed = packed + part_slots[s]
    mine[1] = packed
    whole_slots[pair] = packed
    started(pair_copy)
    finished(pair_copy)
    packed = whole_slots[0]
    for s in range(1, 16):
        packed = packed + whole_slots[s]
    grads_out[...] = packed


def view_table(angles):
    cosine, sine = jnp.cos(angles), jnp.sin(angles)
    first = jnp.arange(X // 128, dtype=F32) * 128.0 - (X - 1) / 2.0
    ends = jnp.minimum(first * cosine[:, None], (first + 127.0) * cosine[:, None])
    least = ends - 3.5 * jnp.abs(sine)[:, None] + (DET - 1) / 2.0
    step = jnp.floor((jnp.floor(least) - (FIRST_COL + 1.0)) / 64.0)
    line = jnp.concatenate(
        [jnp.stack([cosine, sine], axis=1).reshape(-1), step.reshape(-1), jnp.zeros(108, F32)]
    )
    return jnp.broadcast_to(line[None], (8, 128))


VMEM = pl.BlockSpec(memory_space=pltpu.VMEM)
SMEM = pl.BlockSpec(memory_space=pltpu.SMEM)


def shape(dims, dtype=F32):
    return jax.ShapeDtypeStruct(dims, dtype)


def body(sinogram, angles, w_first, b_first, w_second, b_second):
    dma = pltpu.SemaphoreType.DMA
    recv, tables, first_cat, second_cat, second_t = pl.pallas_call(
        exchange_kernel,
        name="exchange",
        out_shape=(
            shape((GROUP, 16, COLS // 2), BF16),
            shape((GROUP, 8, 128)),
            shape((256, 3 * PATCH), BF16),
            shape((256, 3 * PATCH), BF16),
            shape((2 * PATCH, 256), BF16),
        ),
        in_specs=[VMEM] * 5,
        out_specs=[VMEM] * 5,
        scratch_shapes=[
            pltpu.VMEM((GROUP, 16, COLS // 2), BF16),
            dma((GROUP,)),
            dma((GROUP,)),
            dma((GROUP,)),
            dma((GROUP,)),
        ],
        compiler_params=pltpu.CompilerParams(
            collective_id=0, has_side_effects=True, vmem_limit_bytes=32 << 20
        ),
    )(sinogram, view_table(angles), w_first, b_first[None], w_second)
    own = pl.pallas_call(
        backproject_kernel,
        name="backproject",
        out_shape=shape((DEPTH, Y, X)),
        in_specs=[SMEM, VMEM],
        out_specs=VMEM,
        scratch_shapes=[pltpu.VMEM((2, GROUP, 8, COLS), F32)],
        compiler_params=pltpu.CompilerParams(vmem_limit_bytes=32 << 20),
    )(tables[:, 0, :], recv)
    pred, target, grads = pl.pallas_call(
        network_kernel,
        name="network",
        out_shape=(shape((DEPTH, Y, X)), shape((DEPTH, Y, X)), shape((32, 128))),
        in_specs=[VMEM] * 4 + [SMEM],
        out_specs=[VMEM] * 3,
        scratch_shapes=[
            pltpu.VMEM((8, Y, X), F32),
            pltpu.VMEM((SUBS, DEPTH, Y, X), F32),
            pltpu.VMEM((8, 24, X), F32),
            pltpu.VMEM((6, PATCH, X), BF16),
            pltpu.VMEM((6, 256, X), BF16),
            pltpu.VMEM((8, 24, X), F32),
            pltpu.VMEM((8, 24, X), F32),
            pltpu.VMEM((256, PATCH), F32),
            pltpu.VMEM((256, PATCH), F32),
            pltpu.VMEM((16, 32, 128), F32),
            pltpu.VMEM((16, 32, 128), F32),
            pltpu.VMEM((2, 32, 128), F32),
            dma((2,)),
            dma((2,)),
            dma((SUBS,)),
            dma((SUBS,)),
            dma((16,)),
            dma((16,)),
            dma((16,)),
            dma((16,)),
        ],
        compiler_params=pltpu.CompilerParams(
            collective_id=1, has_side_effects=True, vmem_limit_bytes=48 << 20
        ),
    )(own, first_cat, second_cat, second_t, b_second)
    return (
        pred[None],
        target[None],
        grads[0, 64],
        grads[:, :27],
        grads[:, 27],
        grads[:, 32:59],
        grads[0, 65:66],
    )


def solution(mesh):
    finer = Mesh(mesh.devices.reshape(SUBS, 2, SLABS), ("sub", "half", "slab"))
    every = ("sub", "half", "slab")
    return jax.shard_map(
        body,
        mesh=finer,
        in_specs=(P(every, None, None), P(every), P(), P(), P(), P()),
        out_specs=(
            P(("sub", "half"), "slab", None, None),
            P(("sub", "half"), "slab", None, None),
            P(),
            P(),
            P(),
            P(),
            P(),
        ),
        check_vma=False,
    )
```

```python
import math

import jax
import jax.numpy as jnp
from jax import lax
from jax.experimental import pallas as pl
from jax.experimental.pallas import tpu as pltpu
from jax.sharding import Mesh
from jax.sharding import PartitionSpec as P

DET = 2048
X = 1024
Y = 8
CH = 32
DEPTH = 4
SUBS = 8
SLABS = 16
GROUP = 2 * SLABS
VPS = 64
FIRST_COL = 384
COLS = 1280
PATCH = 80
CELLS = float(SUBS * 128 * Y * X)
MESH = pl.DeviceIdType.MESH
F32 = jnp.float32
BF16 = jnp.bfloat16

GATHER = lax.GatherDimensionNumbers(
    offset_dims=(),
    collapsed_slice_dims=(1,),
    start_index_map=(1,),
    operand_batching_dims=(0,),
    start_indices_batching_dims=(0,),
)


def iota(shape, dim):
    return lax.broadcasted_iota(jnp.int32, shape, dim)


def exact_dot(a, b):
    return jnp.dot(a, b, precision=lax.Precision.HIGHEST, preferred_element_type=F32)


def dot_nt(a, b, precision=None):
    return lax.dot_general(
        a, b, (((1,), (1,)), ((), ())), precision=precision, preferred_element_type=F32
    )


def split(value):
    high = value.astype(BF16)
    return high, (value - high.astype(F32)).astype(BF16)


def tap_of(block, shift_y):
    shift_z = (block >= 3).astype(jnp.int32) + (block >= 6).astype(jnp.int32)
    return 6 * shift_z + block + 3 * shift_y


def build_first(w_first, b_first):
    pick = (iota((256, CH), 0) & (CH - 1) == iota((256, CH), 1)).astype(F32)
    rows = exact_dot(pick, w_first)
    bias = jnp.sum(pick * b_first, axis=1, keepdims=True)
    row, col = iota((256, PATCH), 0), iota((256, PATCH), 1)
    out = jnp.where(col == 72, bias, 0.0)
    tap, at = iota((27, PATCH), 0), iota((27, PATCH), 1)
    for shift_y in range(3):
        expand = ((tap == tap_of(at >> 3, shift_y)) & (at < 72)).astype(F32)
        near = (col & 7) - (row >> 5) == shift_y - 1
        out = out + jnp.where(near & (col < 72), exact_dot(rows, expand), 0.0)
    high, low = split(out)
    return jnp.concatenate([high, low, high], axis=1)


def build_second(w_second):
    pick = (iota((256, CH), 0) & (CH - 1) == iota((256, CH), 1)).astype(F32)
    rows = exact_dot(pick, w_second)
    row, col = iota((256, PATCH), 0), iota((256, PATCH), 1)
    pick_t = (iota((CH, 256), 1) & (CH - 1) == iota((CH, 256), 0)).astype(F32)
    row_t, col_t = iota((PATCH, 256), 0), iota((PATCH, 256), 1)
    out = jnp.zeros((256, PATCH), F32)
    out_t = jnp.zeros((PATCH, 256), F32)
    tap, at = iota((27, PATCH), 0), iota((27, PATCH), 1)
    tap_t, at_t = iota((PATCH, 27), 1), iota((PATCH, 27), 0)
    for shift_y in range(3):
        expand = ((tap == tap_of(at >> 3, shift_y)) & (at < 72)).astype(F32)
        near = (row >> 5) - (col & 7) == shift_y - 1
        out = out + jnp.where(near & (col < 72), exact_dot(rows, expand), 0.0)
        expand_t = ((tap_t == tap_of(at_t >> 3, shift_y)) & (at_t < 72)).astype(F32)
        taps_t = dot_nt(expand_t, w_second, lax.Precision.HIGHEST)
        near_t = (col_t >> 5) - (row_t & 7) == shift_y - 1
        out_t = out_t + jnp.where(near_t & (row_t < 72), exact_dot(taps_t, pick_t), 0.0)
    high, low = split(out)
    return jnp.concatenate([high, low, high], axis=1), jnp.concatenate(split(out_t), axis=0)


def build_gather():
    row, lane = iota((1024, 128), 0), iota((1024, 128), 1)
    y, col = row >> 7, row & 127
    block, near = col >> 3, col & 7
    shift = near - y + 1
    inside = (col < 72) & (shift >= 0) & (shift <= 2)
    first = (inside & (lane == tap_of(block, shift))) | ((col == 72) & (lane == 27))
    shift = y - near + 1
    inside = (col < 72) & (shift >= 0) & (shift <= 2)
    second = inside & (lane == tap_of(block, shift) + 32)
    return first.astype(F32).astype(BF16), second.astype(F32).astype(BF16)


def gathered(sums, gather):
    wide = jnp.concatenate([sums[CH * y : CH * y + CH] for y in range(Y)], axis=1)
    high, rest = wide.astype(BF16), wide
    rest = wide - high.astype(F32)
    middle, low = split(rest)
    out = jnp.dot(
        jnp.concatenate([high, middle, low], axis=0), gather, preferred_element_type=F32
    )
    return out[:CH] + (out[CH : 2 * CH] + out[2 * CH :])


def shifted(value, by):
    lane = iota(value.shape, 1)
    if by == 1:
        return jnp.where(lane == 0, 0.0, pltpu.roll(value, 1, 1))
    return jnp.where(lane == X - 1, 0.0, pltpu.roll(value, X - 1, 1))


def take(source, index):
    return lax.gather(
        source, index[..., None], GATHER, (1, 1), mode=lax.GatherScatterMode.PROMISE_IN_BOUNDS
    )


def view_pieces(angles):
    lane, row = iota((8, 128), 1), iota((8, 128), 0)
    angle = jnp.where(lane < 2, angles[0], angles[1])
    value = jnp.where(lane & 1 == 0, jnp.cos(angle), jnp.sin(angle))
    high = value.astype(BF16).astype(F32)
    middle = (value - high).astype(BF16).astype(F32)
    low = value - high - middle
    out = jnp.where(row == 0, high, jnp.where(row == 1, middle, jnp.where(row == 2, low, 0.0)))
    return jnp.where(lane < 4, out, 0.0)


def window_range(part_x):
    ends = (abs(128 * part_x - 511.5), abs(128 * part_x - 384.5))
    middle = (DET - 1) / 2.0
    first = (math.floor(middle - max(ends) - 4.0) - FIRST_COL - 1) // 64
    last = (math.floor(middle + min(ends) + 0.5) - FIRST_COL - 1) // 64
    return first, last


def add_sender(block, windows, out):
    value = block.astype(F32)
    row = jnp.concatenate([value[:8], value[8:]], axis=1)
    moved = pltpu.roll(row, COLS - 64, 1)
    tables = jnp.broadcast_to(value[0:1, :128] + value[1:2, :128] + value[2:3, :128], (8, 128))
    views = [take(tables, jnp.full((8, 128), i, jnp.int32)) for i in range(4)]
    row_index = iota((8, 128), 0)
    row_pos = row_index.astype(F32) - (Y - 1) / 2.0
    lane = iota((8, 128), 1).astype(F32)

    def piece(k):
        source = moved if k & 1 else row
        return source[:, (k >> 1) * 128 : (k >> 1) * 128 + 128]

    steps = []
    for part_x in range(X // 128):
        begin = 128.0 * part_x - (X - 1) / 2.0
        both = []
        for v in range(2):
            cosine, sine = views[2 * v], views[2 * v + 1]
            least = jnp.minimum(begin * cosine, (begin + 127.0) * cosine)
            least = (least - 3.5 * jnp.abs(sine)) + (DET - 1) / 2.0
            both.append(jnp.floor((jnp.floor(least) - (FIRST_COL + 1.0)) * (1.0 / 64.0)))
        steps.append(both)
        step = jnp.where(row_index < 4, both[0], both[1])
        first, last = window_range(part_x)
        near, far = piece(first), piece(first + 2)
        for k in range(first + 1, last + 1):
            reached = step >= float(k)
            near = jnp.where(reached, piece(k), near)
            far = jnp.where(reached, piece(k + 2), far)
        windows[part_x, :, :128] = near
        windows[part_x, :, 128:] = far
    for part_x in range(X // 128):
        here = slice(part_x * 128, (part_x + 1) * 128)
        total = [out[z, :, here] for z in range(DEPTH)]
        for v in range(2):
            cosine, sine = views[2 * v], views[2 * v + 1]
            pos = (
                (lane + (128.0 * part_x - (X - 1) / 2.0)) * cosine + row_pos * sine
            ) + (DET - 1) / 2.0
            lower = jnp.floor(pos)
            part = pos - lower
            w_high = part.astype(BF16).astype(F32)
            w_low = (1.0 - part).astype(BF16).astype(F32)
            index = (lower - (64.0 * steps[part_x][v] + FIRST_COL)).astype(jnp.int32)
            index = jnp.concatenate([index, index], axis=0)
            at_low = (index & 127).astype(jnp.int16)
            at_high = ((index + 1) & 127).astype(jnp.int16)
            whole = index.astype(jnp.int16)
            in_low = whole < jnp.int16(128)
            in_high = whole < jnp.int16(127)
            for pair in range(2):

                def source(offset):
                    parts = [
                        jnp.broadcast_to(
                            windows[part_x, pl.ds(v * 4 + 2 * pair + q, 1), pl.ds(offset, 128)],
                            (8, 128),
                        )
                        for q in range(2)
                    ]
                    return jnp.concatenate(parts, axis=0).astype(BF16)

                near, far = source(0), source(128)
                low = jnp.where(in_low, take(near, at_low), take(far, at_low)).astype(F32)
                high = jnp.where(in_high, take(near, at_high), take(far, at_high)).astype(F32)
                for q in range(2):
                    z = 2 * pair + q
                    half = slice(8 * q, 8 * q + 8)
                    total[z] = total[z] + (w_low * low[half] + w_high * high[half])
        for z in range(DEPTH):
            out[z, :, here] = total[z]


def step_kernel(
    sino,
    angles,
    w_first,
    b_first,
    w_second,
    b_second,
    pred_out,
    target_out,
    grads_out,
    views,
    send,
    recv,
    windows,
    own,
    first_cat,
    second_cat,
    second_t,
    gather_first,
    gather_second,
    field,
    eighths,
    piece,
    totals,
    near_u,
    patch_u,
    hidden_all,
    taps,
    near_r,
    acc_first,
    acc_second,
    part_slots,
    whole_slots,
    mine,
    local_sem,
    data_send,
    data_recv,
    halo_send,
    halo_recv,
    part_send,
    part_recv,
    tot_send,
    tot_recv,
    slab_send,
    slab_recv,
    pair_send,
    pair_recv,
):
    sub, half, slab = lax.axis_index("sub"), lax.axis_index("half"), lax.axis_index("slab")
    me = half * SLABS + slab
    pair = sub * 2 + half

    def ring(other):
        return (sub, other // SLABS, lax.rem(other, SLABS))

    def slab_peer(p):
        other = lax.rem(slab + p, SLABS)
        return other, (sub, half, other)

    def pair_peer(p):
        other = lax.rem(pair + p, 2 * SUBS)
        return other, (other // 2, lax.rem(other, 2), slab)

    def sub_peer(p):
        other = lax.rem(sub + p, SUBS)
        return other, (other, half, slab)

    def group_peer(p):
        other = lax.rem(me + p, GROUP)
        return other, ring(other)

    def greet(peer):
        def step(p, carry):
            pl.semaphore_signal(
                pltpu.get_barrier_semaphore(), inc=1, device_id=peer(p)[1], device_id_type=MESH
            )
            return carry

        return step

    load = pltpu.make_async_copy(
        sino.at[:, :, pl.ds(FIRST_COL, COLS)], views, local_sem.at[0]
    )
    load.start()
    lax.fori_loop(1, GROUP, greet(group_peer), 0)
    lax.fori_loop(1, 2 * SUBS, greet(pair_peer), 0)
    load.wait()

    pieces = view_pieces(angles)
    spare = iota((8, 128), 1) < 4

    def pack(q, carry):
        at = pl.multiple_of(q * 16, 16)
        zero = views[0, pl.ds(at, 16), :].astype(F32)
        one = views[1, pl.ds(at, 16), :].astype(F32)
        for i in range(4):
            both = jnp.concatenate([zero[4 * i : 4 * i + 4], one[4 * i : 4 * i + 4]], axis=0)
            start = jnp.where(spare, pieces, both[:, :128])
            both = jnp.concatenate([start, both[:, 128:]], axis=1)
            send[4 * q + i] = jnp.concatenate(
                [both[:, : COLS // 2], both[:, COLS // 2 :]], axis=0
            ).astype(BF16)
        return carry

    lax.fori_loop(0, GROUP // 4, pack, 0)
    recv[me] = send[me]
    own[...] = jnp.zeros_like(own)
    first_cat[...] = build_first(w_first[...], b_first[...])
    second_cat[...], second_t[...] = build_second(w_second[...])
    gather_first[...], gather_second[...] = build_gather()
    pl.semaphore_wait(pltpu.get_barrier_semaphore(), GROUP - 1 + 2 * SUBS - 1)

    def remote(src, dst, send_sem, recv_sem, target):
        return pltpu.make_async_remote_copy(
            src_ref=src,
            dst_ref=dst,
            send_sem=send_sem,
            recv_sem=recv_sem,
            device_id=target,
            device_id_type=MESH,
        )

    def data_copy(other, slot):
        return remote(
            send.at[other], recv.at[slot], data_send.at[other], data_recv.at[slot], ring(other)
        )

    def start(p, carry):
        other = lax.rem(me + p, GROUP)
        data_copy(other, me).start()
        return carry

    lax.fori_loop(1, GROUP, start, 0)

    def one_sender(p, carry):
        other = lax.rem(me + GROUP - p, GROUP)

        @pl.when(p > 0)
        def _():
            data_copy(other, other).wait_recv()

        add_sender(recv[other], windows, own)
        return carry

    lax.fori_loop(0, GROUP, one_sender, 0)
    own[...] = own[...] * (math.pi / VPS)

    to_after = remote(
        own.at[2:4], field.at[0:2], halo_send.at[0], halo_recv.at[0], group_peer(1)[1]
    )
    to_before = remote(
        own.at[0:2], field.at[6:8], halo_send.at[1], halo_recv.at[1], group_peer(GROUP - 1)[1]
    )
    to_after.start()
    to_before.start()

    def eighth(index):
        return pl.ds(pl.multiple_of(index * 128, 128), 128)

    def part_copy(p, arriving):
        other, target = sub_peer(p)
        slot = other if arriving else sub
        return remote(
            own.at[:, :, eighth(other)],
            eighths.at[slot],
            part_send.at[other],
            part_recv.at[slot],
            target,
        )

    def total_copy(p, arriving):
        other, target = sub_peer(p)
        slot = other if arriving else sub
        return remote(
            piece, totals.at[:, :, eighth(slot)], tot_send.at[other], tot_recv.at[slot], target
        )

    def slab_copy(p, arriving):
        other, target = slab_peer(p)
        slot = other if arriving else slab
        return remote(
            mine.at[0], part_slots.at[slot], slab_send.at[other], slab_recv.at[slot], target
        )

    def pair_copy(p, arriving):
        other, target = pair_peer(p)
        slot = other if arriving else pair
        return remote(
            mine.at[1], whole_slots.at[slot], pair_send.at[other], pair_recv.at[slot], target
        )

    def started(make, count):
        def step(p, carry):
            make(p, False).start()
            return carry

        lax.fori_loop(1, count, step, 0)

    def finished(make, count):
        def step(p, carry):
            make(p, True).wait()
            return carry

        lax.fori_loop(1, count, step, 0)

    started(part_copy, SUBS)
    eighths[sub] = own[:, :, eighth(sub)]
    taps[...] = jnp.zeros_like(taps)
    near_r[...] = jnp.zeros_like(near_r)
    acc_first[...] = jnp.zeros_like(acc_first)
    acc_second[...] = jnp.zeros_like(acc_second)
    ones = (iota((8, X), 0) == 0).astype(F32)

    def place(m, value):
        near_u[m] = jnp.concatenate([shifted(value, 1), value, shifted(value, -1)], axis=0)

    def forward(j, carry):
        patch = jnp.concatenate([near_u[j], near_u[j + 1], near_u[j + 2], ones], axis=0)
        high, low = split(patch)
        patch_u[j] = high
        pre = jnp.dot(
            first_cat[...], jnp.concatenate([high, high, low], axis=0), preferred_element_type=F32
        )
        outside = ((j == 0) & (me == 0)) | ((j == 5) & (me == GROUP - 1))
        hidden = jnp.maximum(pre, 0.0) * jnp.where(outside, 0.0, 1.0)
        high, low = split(hidden)
        hidden_all[j] = high
        main = jnp.dot(second_t[...], high, preferred_element_type=F32)
        rest = jnp.dot(second_t[0:PATCH], low, preferred_element_type=F32)
        added = main[:72] + (main[PATCH : PATCH + 72] + rest[:72])
        for shift_z in range(3):
            at = j - shift_z + 2
            taps[at] = taps[at] + added[24 * shift_z : 24 * shift_z + 24]
        return carry

    for i in range(DEPTH):
        place(i + 2, own[i])
    lax.fori_loop(2, 4, forward, 0)
    finished(part_copy, SUBS)
    total = eighths[0]
    for s in range(1, SUBS):
        total = total + eighths[s]
    piece[...] = total
    totals[:, :, eighth(sub)] = total
    started(total_copy, SUBS)
    to_after.wait()
    to_before.wait()
    for m in range(2):
        place(m, jnp.where(me > 0, field[m], 0.0))
        place(m + 6, jnp.where(me < GROUP - 1, field[m + 6], 0.0))
    lax.fori_loop(0, 2, forward, 0)
    lax.fori_loop(4, 6, forward, 0)
    finished(total_copy, SUBS)

    sum_square = jnp.zeros((8, X), F32)
    sum_resid = jnp.zeros((8, X), F32)
    for i in range(DEPTH):
        value = own[i]
        conv = shifted(taps[i + 2, 0:8], 1) + taps[i + 2, 8:16] + shifted(taps[i + 2, 16:24], -1)
        pred = value + conv + b_second[0]
        target = (totals[i] - value) / (SUBS - 1)
        pred_out[i] = pred
        target_out[i] = target
        diff = pred - target
        resid = (2.0 * diff) / CELLS
        sum_square = sum_square + diff * diff
        sum_resid = sum_resid + resid
        near_r[i + 2] = jnp.concatenate([shifted(resid, -1), resid, shifted(resid, 1)], axis=0)

    nothing = jnp.zeros((8, X), F32)

    def backward(j, carry):
        patch = jnp.concatenate([near_r[j + 2], near_r[j + 1], near_r[j], nothing], axis=0)
        high, low = split(patch)
        grad = jnp.dot(
            second_cat[...], jnp.concatenate([high, high, low], axis=0), preferred_element_type=F32
        )
        hidden = hidden_all[j]
        acc_second[:, :PATCH] += dot_nt(hidden, high)
        grad = jnp.where(hidden.astype(F32) > 0.0, grad, 0.0).astype(BF16)
        acc_first[:, :PATCH] += dot_nt(grad, patch_u[j])
        return carry

    lax.fori_loop(0, 6, backward, 0)

    packed = gathered(acc_first[...], gather_first[...])
    packed = packed + gathered(acc_second[...], gather_second[...])
    packed = packed[:16] + pltpu.roll(packed[16:], 64, 1)
    row, lane = iota((16, 128), 0), iota((16, 128), 1)
    packed = packed + jnp.where((row == 0) & (lane == 60), jnp.sum(sum_square) / CELLS, 0.0)
    packed = packed + jnp.where((row == 0) & (lane == 61), jnp.sum(sum_resid), 0.0)

    mine[0] = packed
    part_slots[slab] = packed
    started(slab_copy, SLABS)
    finished(slab_copy, SLABS)
    packed = part_slots[0]
    for s in range(1, 16):
        packed = packed + part_slots[s]
    mine[1] = packed
    whole_slots[pair] = packed
    started(pair_copy, 2 * SUBS)
    finished(pair_copy, 2 * SUBS)
    packed = whole_slots[0]
    for s in range(1, 16):
        packed = packed + whole_slots[s]
    grads_out[...] = packed

    def sent(p, carry):
        other = lax.rem(me + p, GROUP)
        data_copy(other, me).wait_send()
        return carry

    lax.fori_loop(1, GROUP, sent, 0)


def finish_kernel(pred, target, packed, pred_out, target_out, loss, g_w1, g_b1, g_w2, g_b2, sems):
    copies = [
        pltpu.make_async_copy(pred, pred_out, sems.at[0]),
        pltpu.make_async_copy(target, target_out, sems.at[1]),
    ]
    for copy in copies:
        copy.start()
    value = packed[...]
    both = jnp.concatenate([value, pltpu.roll(value, 64, 1)], axis=0)
    g_w1[...] = both[:, :27]
    g_w2[...] = both[:, 32:59]
    row, lane = iota((CH, 128), 0), iota((CH, 128), 1)
    column = jnp.sum(jnp.where(lane == 27, both, 0.0), axis=1, keepdims=True)
    g_b1[...] = jnp.sum(jnp.where(lane == row, column, 0.0), axis=0, keepdims=True)[:, :CH]
    loss[...] = value[0:1, 60:61]
    g_b2[...] = value[0:1, 61:62]
    for copy in copies:
        copy.wait()


VMEM = pl.BlockSpec(memory_space=pltpu.VMEM)
SMEM = pl.BlockSpec(memory_space=pltpu.SMEM)
ANY = pl.BlockSpec(memory_space=pl.ANY)
HBM = pl.BlockSpec(memory_space=pltpu.HBM)


def shape(dims, dtype=F32):
    return jax.ShapeDtypeStruct(dims, dtype)


def body(sinogram, angles, w_first, b_first, w_second, b_second):
    dma = pltpu.SemaphoreType.DMA
    vmem = pltpu.VMEM
    pred, target, grads = pl.pallas_call(
        step_kernel,
        name="train_step",
        out_shape=(shape((DEPTH, Y, X)), shape((DEPTH, Y, X)), shape((16, 128))),
        in_specs=[HBM, SMEM] + [VMEM] * 3 + [SMEM],
        out_specs=[VMEM] * 3,
        scratch_shapes=[
            vmem((2, 128, COLS), BF16),
            vmem((GROUP, 16, COLS // 2), BF16),
            vmem((GROUP, 16, COLS // 2), BF16),
            vmem((X // 128, 8, 256), F32),
            vmem((DEPTH, Y, X), F32),
            vmem((256, 3 * PATCH), BF16),
            vmem((256, 3 * PATCH), BF16),
            vmem((2 * PATCH, 256), BF16),
            vmem((1024, 128), BF16),
            vmem((1024, 128), BF16),
            vmem((8, Y, X), F32),
            vmem((SUBS, DEPTH, Y, 128), F32),
            vmem((DEPTH, Y, 128), F32),
            vmem((DEPTH, Y, X), F32),
            vmem((8, 24, X), F32),
            vmem((6, PATCH, X), BF16),
            vmem((6, 256, X), BF16),
            vmem((8, 24, X), F32),
            vmem((8, 24, X), F32),
            vmem((256, 128), F32),
            vmem((256, 128), F32),
            vmem((16, 16, 128), F32),
            vmem((16, 16, 128), F32),
            vmem((2, 16, 128), F32),
            dma((1,)),
            dma((GROUP,)),
            dma((GROUP,)),
            dma((2,)),
            dma((2,)),
        ]
        + [dma((SUBS,))] * 4
        + [dma((16,))] * 4,
        compiler_params=pltpu.CompilerParams(
            collective_id=0, has_side_effects=True, vmem_limit_bytes=62 << 20
        ),
    )(sinogram, angles, w_first, b_first[None], w_second, b_second)
    pred, target, loss, g_w1, g_b1, g_w2, g_b2 = pl.pallas_call(
        finish_kernel,
        name="finish",
        out_shape=(
            shape((1, DEPTH, Y, X)),
            shape((1, DEPTH, Y, X)),
            shape((1, 1)),
            shape((CH, 27)),
            shape((1, CH)),
            shape((CH, 27)),
            shape((1, 1)),
        ),
        in_specs=[VMEM] * 3,
        out_specs=[ANY] * 2 + [VMEM] * 5,
        scratch_shapes=[dma((2,))],
        compiler_params=pltpu.CompilerParams(vmem_limit_bytes=62 << 20),
    )(pred[None], target[None], grads)
    return pred, target, loss.reshape(()), g_w1, g_b1.reshape(CH), g_w2, g_b2.reshape(1)


def solution(mesh):
    finer = Mesh(mesh.devices.reshape(SUBS, 2, SLABS), ("sub", "half", "slab"))
    every = ("sub", "half", "slab")
    return jax.shard_map(
        body,
        mesh=finer,
        in_specs=(P(every, None, None), P(every), P(), P(), P(), P()),
        out_specs=(
            P(("sub", "half"), "slab", None, None),
            P(("sub", "half"), "slab", None, None),
            P(),
            P(),
            P(),
            P(),
            P(),
        ),
        check_vma=False,
    )
```

```python
import math

import jax
import jax.numpy as jnp
from jax import lax
from jax.experimental import pallas as pl
from jax.experimental.pallas import tpu as pltpu
from jax.sharding import Mesh
from jax.sharding import PartitionSpec as P

DET = 2048
X = 1024
Y = 8
CH = 32
DEPTH = 4
SUBS = 8
SLABS = 16
GROUP = 2 * SLABS
VPS = 64
FIRST_COL = 384
COLS = 1280
PATCH = 80
CELLS = float(SUBS * 128 * Y * X)
MESH = pl.DeviceIdType.MESH
F32 = jnp.float32
BF16 = jnp.bfloat16

GATHER = lax.GatherDimensionNumbers(
    offset_dims=(),
    collapsed_slice_dims=(1,),
    start_index_map=(1,),
    operand_batching_dims=(0,),
    start_indices_batching_dims=(0,),
)


def iota(shape, dim):
    return lax.broadcasted_iota(jnp.int32, shape, dim)


def exact_dot(a, b):
    return jnp.dot(a, b, precision=lax.Precision.HIGHEST, preferred_element_type=F32)


def dot_nt(a, b, precision=None):
    return lax.dot_general(
        a, b, (((1,), (1,)), ((), ())), precision=precision, preferred_element_type=F32
    )


def split(value):
    high = value.astype(BF16)
    return high, (value - high.astype(F32)).astype(BF16)


def tap_of(block, shift_y):
    shift_z = (block >= 3).astype(jnp.int32) + (block >= 6).astype(jnp.int32)
    return 6 * shift_z + block + 3 * shift_y


def build_first(w_first, b_first):
    pick = (iota((256, CH), 0) & (CH - 1) == iota((256, CH), 1)).astype(F32)
    rows = exact_dot(pick, w_first)
    bias = jnp.sum(pick * b_first, axis=1, keepdims=True)
    row, col = iota((256, PATCH), 0), iota((256, PATCH), 1)
    out = jnp.where(col == 72, bias, 0.0)
    tap, at = iota((27, PATCH), 0), iota((27, PATCH), 1)
    for shift_y in range(3):
        expand = ((tap == tap_of(at >> 3, shift_y)) & (at < 72)).astype(F32)
        near = (col & 7) - (row >> 5) == shift_y - 1
        out = out + jnp.where(near & (col < 72), exact_dot(rows, expand), 0.0)
    high, low = split(out)
    return jnp.concatenate([high, low, high], axis=1)


def build_second(w_second):
    pick = (iota((256, CH), 0) & (CH - 1) == iota((256, CH), 1)).astype(F32)
    rows = exact_dot(pick, w_second)
    row, col = iota((256, PATCH), 0), iota((256, PATCH), 1)
    pick_t = (iota((CH, 256), 1) & (CH - 1) == iota((CH, 256), 0)).astype(F32)
    row_t, col_t = iota((PATCH, 256), 0), iota((PATCH, 256), 1)
    out = jnp.zeros((256, PATCH), F32)
    out_t = jnp.zeros((PATCH, 256), F32)
    tap, at = iota((27, PATCH), 0), iota((27, PATCH), 1)
    tap_t, at_t = iota((PATCH, 27), 1), iota((PATCH, 27), 0)
    for shift_y in range(3):
        expand = ((tap == tap_of(at >> 3, shift_y)) & (at < 72)).astype(F32)
        near = (row >> 5) - (col & 7) == shift_y - 1
        out = out + jnp.where(near & (col < 72), exact_dot(rows, expand), 0.0)
        expand_t = ((tap_t == tap_of(at_t >> 3, shift_y)) & (at_t < 72)).astype(F32)
        taps_t = dot_nt(expand_t, w_second, lax.Precision.HIGHEST)
        near_t = (col_t >> 5) - (row_t & 7) == shift_y - 1
        out_t = out_t + jnp.where(near_t & (row_t < 72), exact_dot(taps_t, pick_t), 0.0)
    high, low = split(out)
    return jnp.concatenate([high, low, high], axis=1), jnp.concatenate(split(out_t), axis=0)


def build_gather():
    row, lane = iota((1024, 128), 0), iota((1024, 128), 1)
    y, col = row >> 7, row & 127
    block, near = col >> 3, col & 7
    shift = near - y + 1
    inside = (col < 72) & (shift >= 0) & (shift <= 2)
    first = (inside & (lane == tap_of(block, shift))) | ((col == 72) & (lane == 27))
    shift = y - near + 1
    inside = (col < 72) & (shift >= 0) & (shift <= 2)
    second = inside & (lane == tap_of(block, shift) + 32)
    return first.astype(F32).astype(BF16), second.astype(F32).astype(BF16)


def gathered(sums, gather):
    wide = jnp.concatenate([sums[CH * y : CH * y + CH] for y in range(Y)], axis=1)
    high, rest = wide.astype(BF16), wide
    rest = wide - high.astype(F32)
    middle, low = split(rest)
    out = jnp.dot(
        jnp.concatenate([high, middle, low], axis=0), gather, preferred_element_type=F32
    )
    return out[:CH] + (out[CH : 2 * CH] + out[2 * CH :])


def shifted(value, by):
    lane = iota(value.shape, 1)
    if by == 1:
        return jnp.where(lane == 0, 0.0, pltpu.roll(value, 1, 1))
    return jnp.where(lane == X - 1, 0.0, pltpu.roll(value, X - 1, 1))


def take(source, index):
    return lax.gather(
        source, index[..., None], GATHER, (1, 1), mode=lax.GatherScatterMode.PROMISE_IN_BOUNDS
    )


def view_pieces(angles):
    lane, row = iota((8, 128), 1), iota((8, 128), 0)
    angle = jnp.where(lane < 2, angles[0], angles[1])
    value = jnp.where(lane & 1 == 0, jnp.cos(angle), jnp.sin(angle))
    high = value.astype(BF16).astype(F32)
    middle = (value - high).astype(BF16).astype(F32)
    low = value - high - middle
    out = jnp.where(row == 0, high, jnp.where(row == 1, middle, jnp.where(row == 2, low, 0.0)))
    return jnp.where(lane < 4, out, 0.0)


def window_range(part_x):
    ends = (abs(128 * part_x - 511.5), abs(128 * part_x - 384.5))
    middle = (DET - 1) / 2.0
    first = (math.floor(middle - max(ends) - 4.0) - FIRST_COL - 1) // 64
    last = (math.floor(middle + min(ends) + 0.5) - FIRST_COL - 1) // 64
    return first, last


def add_sender(block, windows, out):
    value = block.astype(F32)
    row = jnp.concatenate([value[:8], value[8:]], axis=1)
    moved = pltpu.roll(row, COLS - 64, 1)
    tables = jnp.broadcast_to(value[0:1, :128] + value[1:2, :128] + value[2:3, :128], (8, 128))
    views = [take(tables, jnp.full((8, 128), i, jnp.int32)) for i in range(4)]
    row_index = iota((8, 128), 0)
    row_pos = row_index.astype(F32) - (Y - 1) / 2.0
    lane = iota((8, 128), 1).astype(F32)

    def piece(k):
        source = moved if k & 1 else row
        return source[:, (k >> 1) * 128 : (k >> 1) * 128 + 128]

    steps = []
    for part_x in range(X // 128):
        begin = 128.0 * part_x - (X - 1) / 2.0
        both = []
        for v in range(2):
            cosine, sine = views[2 * v], views[2 * v + 1]
            least = jnp.minimum(begin * cosine, (begin + 127.0) * cosine)
            least = (least - 3.5 * jnp.abs(sine)) + (DET - 1) / 2.0
            both.append(jnp.floor((jnp.floor(least) - (FIRST_COL + 1.0)) * (1.0 / 64.0)))
        steps.append(both)
        step = jnp.where(row_index < 4, both[0], both[1])
        first, last = window_range(part_x)
        near, far = piece(first), piece(first + 2)
        for k in range(first + 1, last + 1):
            reached = step >= float(k)
            near = jnp.where(reached, piece(k), near)
            far = jnp.where(reached, piece(k + 2), far)
        windows[part_x, :, :128] = near
        windows[part_x, :, 128:] = far
    for part_x in range(X // 128):
        here = slice(part_x * 128, (part_x + 1) * 128)
        total = [out[z, :, here] for z in range(DEPTH)]
        for v in range(2):
            cosine, sine = views[2 * v], views[2 * v + 1]
            pos = (
                (lane + (128.0 * part_x - (X - 1) / 2.0)) * cosine + row_pos * sine
            ) + (DET - 1) / 2.0
            lower = jnp.floor(pos)
            part = pos - lower
            w_high = part.astype(BF16).astype(F32)
            w_low = (1.0 - part).astype(BF16).astype(F32)
            index = (lower - (64.0 * steps[part_x][v] + FIRST_COL)).astype(jnp.int32)
            index = jnp.concatenate([index, index], axis=0)
            at_low = (index & 127).astype(jnp.int16)
            at_high = ((index + 1) & 127).astype(jnp.int16)
            whole = index.astype(jnp.int16)
            in_low = whole < jnp.int16(128)
            in_high = whole < jnp.int16(127)
            for pair in range(2):

                def source(offset):
                    parts = [
                        jnp.broadcast_to(
                            windows[part_x, pl.ds(v * 4 + 2 * pair + q, 1), pl.ds(offset, 128)],
                            (8, 128),
                        )
                        for q in range(2)
                    ]
                    return jnp.concatenate(parts, axis=0).astype(BF16)

                near, far = source(0), source(128)
                low = jnp.where(in_low, take(near, at_low), take(far, at_low)).astype(F32)
                high = jnp.where(in_high, take(near, at_high), take(far, at_high)).astype(F32)
                for q in range(2):
                    z = 2 * pair + q
                    half = slice(8 * q, 8 * q + 8)
                    total[z] = total[z] + (w_low * low[half] + w_high * high[half])
        for z in range(DEPTH):
            out[z, :, here] = total[z]


def step_kernel(
    sino,
    angles,
    w_first,
    b_first,
    w_second,
    b_second,
    pred_out,
    target_out,
    grads_out,
    views,
    send,
    recv,
    windows,
    own,
    first_cat,
    second_cat,
    second_t,
    gather_first,
    gather_second,
    field,
    eighths,
    piece,
    totals,
    near_u,
    patch_u,
    hidden_all,
    taps,
    near_r,
    acc_first,
    acc_second,
    part_slots,
    whole_slots,
    mine,
    local_sem,
    data_send,
    data_recv,
    halo_send,
    halo_recv,
    part_send,
    part_recv,
    tot_send,
    tot_recv,
    slab_send,
    slab_recv,
    pair_send,
    pair_recv,
):
    sub, half, slab = lax.axis_index("sub"), lax.axis_index("half"), lax.axis_index("slab")
    me = half * SLABS + slab
    pair = sub * 2 + half

    def ring(other):
        return (sub, other >> 4, other & 15)

    far_first = (2, 1, 3, 0)

    def slab_peer(p):
        y = ((slab >> 2) + far_first[p >> 2]) & 3
        other = y * 4 + ((slab + far_first[p & 3]) & 3)
        return other, (sub, half, other)

    def sub_at(p):
        x = ((sub >> 1) + far_first[p >> 1]) & 3
        return x * 2 + ((sub + 1 + p) & 1)

    def pair_peer(p):
        other_sub, other_half = sub_at(p >> 1), (half + 1 + p) & 1
        return other_sub * 2 + other_half, (other_sub, other_half, slab)

    def sub_peer(p):
        other = sub_at(p)
        return other, (other, half, slab)

    def distance(p):
        if p < 8:
            return p & 1, p >> 1, 0
        q = p - 8
        return (q // 3) & 1, q // 6, far_first[q % 3]

    def group_target(p):
        core, y, z = distance(p)
        return ((half + core) & 1) * SLABS + (((slab >> 2) + y) & 3) * 4 + ((slab + z) & 3)

    def group_source(p):
        q = p - 8
        third = lax.rem(q, 3)
        near = p < 8
        core = jnp.where(near, p, q // 3) & 1
        y = jnp.where(near, p >> 1, q // 6)
        z = jnp.where(near, 0, jnp.where(third == 0, 2, jnp.where(third == 1, 1, 3)))
        row = ((slab >> 2) + 4 - y) & 3
        return ((half + core) & 1) * SLABS + row * 4 + ((slab + 4 - z) & 3)

    def group_peer(p):
        other = group_target(GROUP - 1 - p)
        return other, ring(other)

    def greet(peer, count):
        for p in range(count - 1):
            pl.semaphore_signal(
                pltpu.get_barrier_semaphore(), inc=1, device_id=peer(p)[1], device_id_type=MESH
            )

    load = pltpu.make_async_copy(
        sino.at[:, :, pl.ds(FIRST_COL, COLS)], views, local_sem.at[0]
    )
    load.start()
    greet(group_peer, GROUP)
    greet(pair_peer, 2 * SUBS)
    load.wait()

    pieces = view_pieces(angles)
    spare = iota((8, 128), 1) < 4

    def pack(q, carry):
        at = pl.multiple_of(q * 16, 16)
        zero = views[0, pl.ds(at, 16), :].astype(F32)
        one = views[1, pl.ds(at, 16), :].astype(F32)
        for i in range(4):
            both = jnp.concatenate([zero[4 * i : 4 * i + 4], one[4 * i : 4 * i + 4]], axis=0)
            start = jnp.where(spare, pieces, both[:, :128])
            both = jnp.concatenate([start, both[:, 128:]], axis=1)
            send[4 * q + i] = jnp.concatenate(
                [both[:, : COLS // 2], both[:, COLS // 2 :]], axis=0
            ).astype(BF16)
        return carry

    lax.fori_loop(0, GROUP // 4, pack, 0)
    recv[me] = send[me]
    own[...] = jnp.zeros_like(own)
    first_cat[...] = build_first(w_first[...], b_first[...])
    second_cat[...], second_t[...] = build_second(w_second[...])
    gather_first[...], gather_second[...] = build_gather()
    pl.semaphore_wait(pltpu.get_barrier_semaphore(), GROUP - 1 + 2 * SUBS - 1)

    def remote(src, dst, send_sem, recv_sem, target):
        return pltpu.make_async_remote_copy(
            src_ref=src,
            dst_ref=dst,
            send_sem=send_sem,
            recv_sem=recv_sem,
            device_id=target,
            device_id_type=MESH,
        )

    def data_copy(other, slot):
        return remote(
            send.at[other], recv.at[slot], data_send.at[other], data_recv.at[slot], ring(other)
        )

    for p in range(1, GROUP):
        data_copy(group_target(p), me).start()

    def one_sender(p, carry):
        other = group_source(p)

        @pl.when(p > 0)
        def _():
            data_copy(other, other).wait_recv()

        add_sender(recv[other], windows, own)
        return carry

    lax.fori_loop(0, GROUP, one_sender, 0)
    own[...] = own[...] * (math.pi / VPS)

    to_after = remote(
        own.at[2:4], field.at[0:2], halo_send.at[0], halo_recv.at[0], ring(lax.rem(me + 1, GROUP))
    )
    to_before = remote(
        own.at[0:2], field.at[6:8], halo_send.at[1], halo_recv.at[1], ring(lax.rem(me + GROUP - 1, GROUP))
    )

    def eighth(index):
        return pl.ds(pl.multiple_of(index * 128, 128), 128)

    def part_copy(p, arriving):
        other, target = sub_peer(p)
        slot = other if arriving else sub
        return remote(
            own.at[:, :, eighth(other)],
            eighths.at[slot],
            part_send.at[other],
            part_recv.at[slot],
            target,
        )

    def total_copy(p, arriving):
        other, target = sub_peer(p)
        slot = other if arriving else sub
        return remote(
            piece, totals.at[:, :, eighth(slot)], tot_send.at[other], tot_recv.at[slot], target
        )

    def slab_copy(p, arriving):
        other, target = slab_peer(p)
        slot = other if arriving else slab
        return remote(
            mine.at[0], part_slots.at[slot], slab_send.at[other], slab_recv.at[slot], target
        )

    def pair_copy(p, arriving):
        other, target = pair_peer(p)
        slot = other if arriving else pair
        return remote(
            mine.at[1], whole_slots.at[slot], pair_send.at[other], pair_recv.at[slot], target
        )

    def started(make, count):
        for p in range(count - 1):
            make(p, False).start()

    def finished(make, count):
        for p in range(count - 1):
            make(p, True).wait()

    started(part_copy, SUBS)
    to_after.start()
    to_before.start()
    eighths[sub] = own[:, :, eighth(sub)]
    taps[...] = jnp.zeros_like(taps)
    near_r[...] = jnp.zeros_like(near_r)
    acc_first[...] = jnp.zeros_like(acc_first)
    acc_second[...] = jnp.zeros_like(acc_second)
    ones = (iota((8, X), 0) == 0).astype(F32)

    def place(m, value):
        near_u[m] = jnp.concatenate([shifted(value, 1), value, shifted(value, -1)], axis=0)

    def forward(j, carry):
        patch = jnp.concatenate([near_u[j], near_u[j + 1], near_u[j + 2], ones], axis=0)
        high, low = split(patch)
        patch_u[j] = high
        pre = jnp.dot(
            first_cat[...], jnp.concatenate([high, high, low], axis=0), preferred_element_type=F32
        )
        outside = ((j == 0) & (me == 0)) | ((j == 5) & (me == GROUP - 1))
        hidden = jnp.maximum(pre, 0.0) * jnp.where(outside, 0.0, 1.0)
        high, low = split(hidden)
        hidden_all[j] = high
        main = jnp.dot(second_t[...], high, preferred_element_type=F32)
        rest = jnp.dot(second_t[0:PATCH], low, preferred_element_type=F32)
        added = main[:72] + (main[PATCH : PATCH + 72] + rest[:72])
        for shift_z in range(3):
            at = j - shift_z + 2
            taps[at] = taps[at] + added[24 * shift_z : 24 * shift_z + 24]
        return carry

    for i in range(DEPTH):
        place(i + 2, own[i])
    lax.fori_loop(2, 4, forward, 0)
    finished(part_copy, SUBS)
    total = eighths[0]
    for s in range(1, SUBS):
        total = total + eighths[s]
    piece[...] = total
    totals[:, :, eighth(sub)] = total
    started(total_copy, SUBS)
    to_after.wait()
    to_before.wait()
    for m in range(2):
        place(m, jnp.where(me > 0, field[m], 0.0))
        place(m + 6, jnp.where(me < GROUP - 1, field[m + 6], 0.0))
    lax.fori_loop(0, 2, forward, 0)
    lax.fori_loop(4, 6, forward, 0)
    finished(total_copy, SUBS)

    sum_square = jnp.zeros((8, X), F32)
    sum_resid = jnp.zeros((8, X), F32)
    for i in range(DEPTH):
        value = own[i]
        conv = shifted(taps[i + 2, 0:8], 1) + taps[i + 2, 8:16] + shifted(taps[i + 2, 16:24], -1)
        pred = value + conv + b_second[0]
        target = (totals[i] - value) / (SUBS - 1)
        pred_out[i] = pred
        target_out[i] = target
        diff = pred - target
        resid = (2.0 * diff) / CELLS
        sum_square = sum_square + diff * diff
        sum_resid = sum_resid + resid
        near_r[i + 2] = jnp.concatenate([shifted(resid, -1), resid, shifted(resid, 1)], axis=0)

    nothing = jnp.zeros((8, X), F32)

    def backward(j, carry):
        patch = jnp.concatenate([near_r[j + 2], near_r[j + 1], near_r[j], nothing], axis=0)
        high, low = split(patch)
        grad = jnp.dot(
            second_cat[...], jnp.concatenate([high, high, low], axis=0), preferred_element_type=F32
        )
        hidden = hidden_all[j]
        acc_second[:, :PATCH] += dot_nt(hidden, high)
        grad = jnp.where(hidden.astype(F32) > 0.0, grad, 0.0).astype(BF16)
        acc_first[:, :PATCH] += dot_nt(grad, patch_u[j])
        return carry

    lax.fori_loop(0, 6, backward, 0, unroll=2)

    packed = gathered(acc_first[...], gather_first[...])
    packed = packed + gathered(acc_second[...], gather_second[...])
    packed = packed[:16] + pltpu.roll(packed[16:], 64, 1)
    row, lane = iota((16, 128), 0), iota((16, 128), 1)
    packed = packed + jnp.where((row == 0) & (lane == 60), jnp.sum(sum_square) / CELLS, 0.0)
    packed = packed + jnp.where((row == 0) & (lane == 61), jnp.sum(sum_resid), 0.0)

    mine[0] = packed
    part_slots[slab] = packed
    started(slab_copy, SLABS)
    finished(slab_copy, SLABS)
    packed = part_slots[0]
    for s in range(1, 16):
        packed = packed + part_slots[s]
    mine[1] = packed
    whole_slots[pair] = packed
    started(pair_copy, 2 * SUBS)
    finished(pair_copy, 2 * SUBS)
    packed = whole_slots[0]
    for s in range(1, 16):
        packed = packed + whole_slots[s]
    grads_out[...] = packed

    def sent(p, carry):
        other = lax.rem(me + p, GROUP)
        data_copy(other, me).wait_send()
        return carry

    lax.fori_loop(1, GROUP, sent, 0)


def finish_kernel(pred, target, packed, pred_out, target_out, loss, g_w1, g_b1, g_w2, g_b2, sems):
    copies = [
        pltpu.make_async_copy(pred, pred_out, sems.at[0]),
        pltpu.make_async_copy(target, target_out, sems.at[1]),
    ]
    for copy in copies:
        copy.start()
    value = packed[...]
    both = jnp.concatenate([value, pltpu.roll(value, 64, 1)], axis=0)
    g_w1[...] = both[:, :27]
    g_w2[...] = both[:, 32:59]
    row, lane = iota((CH, 128), 0), iota((CH, 128), 1)
    column = jnp.sum(jnp.where(lane == 27, both, 0.0), axis=1, keepdims=True)
    g_b1[...] = jnp.sum(jnp.where(lane == row, column, 0.0), axis=0, keepdims=True)[:, :CH]
    loss[...] = value[0:1, 60:61]
    g_b2[...] = value[0:1, 61:62]
    for copy in copies:
        copy.wait()


VMEM = pl.BlockSpec(memory_space=pltpu.VMEM)
SMEM = pl.BlockSpec(memory_space=pltpu.SMEM)
ANY = pl.BlockSpec(memory_space=pl.ANY)
HBM = pl.BlockSpec(memory_space=pltpu.HBM)


def shape(dims, dtype=F32):
    return jax.ShapeDtypeStruct(dims, dtype)


def body(sinogram, angles, w_first, b_first, w_second, b_second):
    dma = pltpu.SemaphoreType.DMA
    vmem = pltpu.VMEM
    pred, target, grads = pl.pallas_call(
        step_kernel,
        name="train_step",
        out_shape=(shape((DEPTH, Y, X)), shape((DEPTH, Y, X)), shape((16, 128))),
        in_specs=[HBM, SMEM] + [VMEM] * 3 + [SMEM],
        out_specs=[VMEM] * 3,
        scratch_shapes=[
            vmem((2, 128, COLS), BF16),
            vmem((GROUP, 16, COLS // 2), BF16),
            vmem((GROUP, 16, COLS // 2), BF16),
            vmem((X // 128, 8, 256), F32),
            vmem((DEPTH, Y, X), F32),
            vmem((256, 3 * PATCH), BF16),
            vmem((256, 3 * PATCH), BF16),
            vmem((2 * PATCH, 256), BF16),
            vmem((1024, 128), BF16),
            vmem((1024, 128), BF16),
            vmem((8, Y, X), F32),
            vmem((SUBS, DEPTH, Y, 128), F32),
            vmem((DEPTH, Y, 128), F32),
            vmem((DEPTH, Y, X), F32),
            vmem((8, 24, X), F32),
            vmem((6, PATCH, X), BF16),
            vmem((6, 256, X), BF16),
            vmem((8, 24, X), F32),
            vmem((8, 24, X), F32),
            vmem((256, 128), F32),
            vmem((256, 128), F32),
            vmem((16, 16, 128), F32),
            vmem((16, 16, 128), F32),
            vmem((2, 16, 128), F32),
            dma((1,)),
            dma((GROUP,)),
            dma((GROUP,)),
            dma((2,)),
            dma((2,)),
        ]
        + [dma((SUBS,))] * 4
        + [dma((16,))] * 4,
        compiler_params=pltpu.CompilerParams(
            collective_id=0, has_side_effects=True, vmem_limit_bytes=62 << 20
        ),
    )(sinogram, angles, w_first, b_first[None], w_second, b_second)
    pred, target, loss, g_w1, g_b1, g_w2, g_b2 = pl.pallas_call(
        finish_kernel,
        name="finish",
        out_shape=(
            shape((1, DEPTH, Y, X)),
            shape((1, DEPTH, Y, X)),
            shape((1, 1)),
            shape((CH, 27)),
            shape((1, CH)),
            shape((CH, 27)),
            shape((1, 1)),
        ),
        in_specs=[VMEM] * 3,
        out_specs=[ANY] * 2 + [VMEM] * 5,
        scratch_shapes=[dma((2,))],
        compiler_params=pltpu.CompilerParams(vmem_limit_bytes=62 << 20),
    )(pred[None], target[None], grads)
    return pred, target, loss.reshape(()), g_w1, g_b1.reshape(CH), g_w2, g_b2.reshape(1)


def solution(mesh):
    finer = Mesh(mesh.devices.reshape(SUBS, 2, SLABS), ("sub", "half", "slab"))
    every = ("sub", "half", "slab")
    return jax.shard_map(
        body,
        mesh=finer,
        in_specs=(P(every, None, None), P(every), P(), P(), P(), P()),
        out_specs=(
            P(("sub", "half"), "slab", None, None),
            P(("sub", "half"), "slab", None, None),
            P(),
            P(),
            P(),
            P(),
            P(),
        ),
        check_vma=False,
    )
```

```python
import math

import jax
import jax.numpy as jnp
from jax import lax
from jax.experimental import pallas as pl
from jax.experimental.pallas import tpu as pltpu
from jax.sharding import Mesh
from jax.sharding import PartitionSpec as P

DET = 2048
X = 1024
Y = 8
CH = 32
DEPTH = 4
SUBS = 8
SLABS = 16
GROUP = 2 * SLABS
VPS = 64
FIRST_COL = 384
COLS = 1280
PATCH = 80
CELLS = float(SUBS * 128 * Y * X)
MESH = pl.DeviceIdType.MESH
F32 = jnp.float32
BF16 = jnp.bfloat16

GATHER = lax.GatherDimensionNumbers(
    offset_dims=(),
    collapsed_slice_dims=(1,),
    start_index_map=(1,),
    operand_batching_dims=(0,),
    start_indices_batching_dims=(0,),
)


def iota(shape, dim):
    return lax.broadcasted_iota(jnp.int32, shape, dim)


def exact_dot(a, b):
    return jnp.dot(a, b, precision=lax.Precision.HIGHEST, preferred_element_type=F32)


def dot_nt(a, b, precision=None):
    return lax.dot_general(
        a, b, (((1,), (1,)), ((), ())), precision=precision, preferred_element_type=F32
    )


def split(value):
    high = value.astype(BF16)
    return high, (value - high.astype(F32)).astype(BF16)


def tap_of(block, shift_y):
    shift_z = (block >= 3).astype(jnp.int32) + (block >= 6).astype(jnp.int32)
    return 6 * shift_z + block + 3 * shift_y


def build_first(w_first, b_first):
    pick = (iota((256, CH), 0) & (CH - 1) == iota((256, CH), 1)).astype(F32)
    rows = exact_dot(pick, w_first)
    bias = jnp.sum(pick * b_first, axis=1, keepdims=True)
    row, col = iota((256, PATCH), 0), iota((256, PATCH), 1)
    out = jnp.where(col == 72, bias, 0.0)
    tap, at = iota((27, PATCH), 0), iota((27, PATCH), 1)
    for shift_y in range(3):
        expand = ((tap == tap_of(at >> 3, shift_y)) & (at < 72)).astype(F32)
        near = (col & 7) - (row >> 5) == shift_y - 1
        out = out + jnp.where(near & (col < 72), exact_dot(rows, expand), 0.0)
    high, low = split(out)
    return jnp.concatenate([high, low, high], axis=1)


def build_second(w_second):
    pick = (iota((256, CH), 0) & (CH - 1) == iota((256, CH), 1)).astype(F32)
    rows = exact_dot(pick, w_second)
    row, col = iota((256, PATCH), 0), iota((256, PATCH), 1)
    pick_t = (iota((CH, 256), 1) & (CH - 1) == iota((CH, 256), 0)).astype(F32)
    row_t, col_t = iota((PATCH, 256), 0), iota((PATCH, 256), 1)
    out = jnp.zeros((256, PATCH), F32)
    out_t = jnp.zeros((PATCH, 256), F32)
    tap, at = iota((27, PATCH), 0), iota((27, PATCH), 1)
    tap_t, at_t = iota((PATCH, 27), 1), iota((PATCH, 27), 0)
    for shift_y in range(3):
        expand = ((tap == tap_of(at >> 3, shift_y)) & (at < 72)).astype(F32)
        near = (row >> 5) - (col & 7) == shift_y - 1
        out = out + jnp.where(near & (col < 72), exact_dot(rows, expand), 0.0)
        expand_t = ((tap_t == tap_of(at_t >> 3, shift_y)) & (at_t < 72)).astype(F32)
        taps_t = dot_nt(expand_t, w_second, lax.Precision.HIGHEST)
        near_t = (col_t >> 5) - (row_t & 7) == shift_y - 1
        out_t = out_t + jnp.where(near_t & (row_t < 72), exact_dot(taps_t, pick_t), 0.0)
    high, low = split(out)
    return jnp.concatenate([high, low, high], axis=1), jnp.concatenate(split(out_t), axis=0)


def build_gather():
    row, lane = iota((1024, 128), 0), iota((1024, 128), 1)
    y, col = row >> 7, row & 127
    block, near = col >> 3, col & 7
    shift = near - y + 1
    inside = (col < 72) & (shift >= 0) & (shift <= 2)
    first = (inside & (lane == tap_of(block, shift))) | ((col == 72) & (lane == 27))
    shift = y - near + 1
    inside = (col < 72) & (shift >= 0) & (shift <= 2)
    second = inside & (lane == tap_of(block, shift) + 32)
    return first.astype(F32).astype(BF16), second.astype(F32).astype(BF16)


def gathered(sums, gather):
    wide = jnp.concatenate([sums[CH * y : CH * y + CH] for y in range(Y)], axis=1)
    high, rest = wide.astype(BF16), wide
    rest = wide - high.astype(F32)
    middle, low = split(rest)
    out = jnp.dot(
        jnp.concatenate([high, middle, low], axis=0), gather, preferred_element_type=F32
    )
    return out[:CH] + (out[CH : 2 * CH] + out[2 * CH :])


def shifted(value, by):
    lane = iota(value.shape, 1)
    if by == 1:
        return jnp.where(lane == 0, 0.0, pltpu.roll(value, 1, 1))
    return jnp.where(lane == X - 1, 0.0, pltpu.roll(value, X - 1, 1))


def take(source, index):
    return lax.gather(
        source, index[..., None], GATHER, (1, 1), mode=lax.GatherScatterMode.PROMISE_IN_BOUNDS
    )


def view_table(angles):
    lane, row = iota((8, 128), 1), iota((8, 128), 0)
    angle = jnp.where(lane < 2, angles[0], angles[1])
    value = jnp.where(lane & 1 == 0, jnp.cos(angle), jnp.sin(angle))
    return jnp.where((row == 0) & (lane < 4), value, 0.0)


def every_lane(source, index):
    return take(source, jnp.full((8, 128), index, jnp.int32))


def window_range(part_x):
    ends = (abs(128 * part_x - 511.5), abs(128 * part_x - 384.5))
    middle = (DET - 1) / 2.0
    first = (math.floor(middle - max(ends) - 4.0) - FIRST_COL) // 64
    last = (math.floor(middle + min(ends) + 0.5) - FIRST_COL) // 64
    return first, last


def add_sender(block, extra, windows, out):
    value = block.astype(F32)
    tables = jnp.broadcast_to(extra, (8, 128))
    ends = [take(tables, iota((8, 128), 0) + at) for at in (8, 16)]
    row = jnp.concatenate([ends[0], value[:8], value[8:], ends[1]], axis=1)
    moved = pltpu.roll(row, COLS - 64, 1)
    views = [every_lane(tables, i) for i in range(4)]
    row_index = iota((8, 128), 0)
    row_pos = row_index.astype(F32) - (Y - 1) / 2.0
    lane = iota((8, 128), 1).astype(F32)

    def piece(k):
        source = moved if k & 1 else row
        return source[:, (k >> 1) * 128 : (k >> 1) * 128 + 128]

    lowest = []
    for part_x in range(X // 128):
        begin = 128.0 * part_x - (X - 1) / 2.0
        both = []
        for v in range(2):
            cosine, sine = views[2 * v], views[2 * v + 1]
            least = jnp.minimum(begin * cosine, (begin + 127.0) * cosine)
            both.append(jnp.floor((least - 3.5 * jnp.abs(sine)) + (DET - 1) / 2.0))
        lowest.append(both)
        offset = jnp.where(row_index < 4, both[0], both[1]) - float(FIRST_COL)
        step = jnp.floor(offset * (1.0 / 64.0))
        first, last = window_range(part_x)
        near, far = piece(first), piece(first + 2)
        for k in range(first + 1, last + 1):
            reached = step >= float(k)
            near = jnp.where(reached, piece(k), near)
            far = jnp.where(reached, piece(k + 2), far)
        moved_by = (offset - 64.0 * step).astype(jnp.int32)
        place = moved_by + iota((8, 128), 1)
        at = place & 127
        window = [
            jnp.where(place < 128, take(near, at), take(far, at)),
            take(far, moved_by),
            take(far, moved_by + 1),
        ]
        windows[part_x] = jnp.concatenate(window, axis=1)
    for part_x in range(X // 128):
        here = slice(part_x * 128, (part_x + 1) * 128)
        total = [out[z, :, here] for z in range(DEPTH)]
        for v in range(2):
            cosine, sine = views[2 * v], views[2 * v + 1]
            pos = (
                (lane + (128.0 * part_x - (X - 1) / 2.0)) * cosine + row_pos * sine
            ) + (DET - 1) / 2.0
            lower = jnp.floor(pos)
            part = pos - lower
            w_high = part.astype(BF16).astype(F32)
            w_low = (1.0 - part).astype(BF16).astype(F32)
            index = (lower - lowest[part_x][v]).astype(jnp.int32)
            index = jnp.concatenate([index, index], axis=0)
            at_low = (index & 127).astype(jnp.int16)
            at_high = ((index + 1) & 127).astype(jnp.int16)
            whole = index.astype(jnp.int16)
            in_low = whole < jnp.int16(128)
            in_high = whole < jnp.int16(127)
            for pair in range(2):

                def source(offset):
                    first_row = v * 4 + 2 * pair
                    parts = [
                        jnp.broadcast_to(
                            windows[part_x, pl.ds(first_row + q, 1), pl.ds(offset, 128)], (8, 128)
                        )
                        for q in range(2)
                    ]
                    return jnp.concatenate(parts, axis=0).astype(BF16)

                near, next_one, after = source(0), source(128), source(256)
                low = jnp.where(in_low, take(near, at_low), next_one).astype(F32)
                high = jnp.where(in_low, next_one, after)
                high = jnp.where(in_high, take(near, at_high), high).astype(F32)
                for q in range(2):
                    z = 2 * pair + q
                    half = slice(8 * q, 8 * q + 8)
                    total[z] = total[z] + (w_low * low[half] + w_high * high[half])
        for z in range(DEPTH):
            out[z, :, here] = total[z]


def step_kernel(
    sino,
    angles,
    w_first,
    b_first,
    w_second,
    b_second,
    pred_out,
    target_out,
    grads_out,
    views,
    send,
    recv,
    send_extra,
    recv_extra,
    windows,
    own,
    first_cat,
    second_cat,
    second_t,
    gather_first,
    gather_second,
    field,
    eighths,
    piece,
    totals,
    near_u,
    patch_u,
    hidden_all,
    taps,
    near_r,
    acc_first,
    acc_second,
    part_slots,
    whole_slots,
    mine,
    local_sem,
    data_send,
    data_recv,
    extra_send,
    extra_recv,
    halo_send,
    halo_recv,
    part_send,
    part_recv,
    tot_send,
    tot_recv,
    slab_send,
    slab_recv,
    pair_send,
    pair_recv,
):
    sub, half, slab = lax.axis_index("sub"), lax.axis_index("half"), lax.axis_index("slab")
    me = half * SLABS + slab
    pair = sub * 2 + half

    def ring(other):
        return (sub, other >> 4, other & 15)

    far_first = (2, 1, 3, 0)

    def slab_peer(p):
        y = ((slab >> 2) + far_first[p >> 2]) & 3
        other = y * 4 + ((slab + far_first[p & 3]) & 3)
        return other, (sub, half, other)

    def sub_at(p):
        x = ((sub >> 1) + far_first[p >> 1]) & 3
        return x * 2 + ((sub + 1 + p) & 1)

    def pair_peer(p):
        other_sub, other_half = sub_at(p >> 1), (half + 1 + p) & 1
        return other_sub * 2 + other_half, (other_sub, other_half, slab)

    def sub_peer(p):
        other = sub_at(p)
        return other, (other, half, slab)

    def distance(p):
        if p < 8:
            return p & 1, p >> 1, 0
        q = p - 8
        return (q // 3) & 1, q // 6, far_first[q % 3]

    def group_target(p):
        core, y, z = distance(p)
        return ((half + core) & 1) * SLABS + (((slab >> 2) + y) & 3) * 4 + ((slab + z) & 3)

    def group_source(p):
        q = p - 8
        third = lax.rem(q, 3)
        near = p < 8
        core = jnp.where(near, p, q // 3) & 1
        y = jnp.where(near, p >> 1, q // 6)
        z = jnp.where(near, 0, jnp.where(third == 0, 2, jnp.where(third == 1, 1, 3)))
        row = ((slab >> 2) + 4 - y) & 3
        return ((half + core) & 1) * SLABS + row * 4 + ((slab + 4 - z) & 3)

    def group_peer(p):
        other = group_target(GROUP - 1 - p)
        return other, ring(other)

    def greet(peer, count):
        for p in range(count - 1):
            pl.semaphore_signal(
                pltpu.get_barrier_semaphore(), inc=1, device_id=peer(p)[1], device_id_type=MESH
            )

    load = pltpu.make_async_copy(
        sino.at[:, :, pl.ds(FIRST_COL, COLS)], views, local_sem.at[0]
    )
    load.start()
    greet(group_peer, GROUP)
    greet(pair_peer, 2 * SUBS)
    load.wait()

    table = view_table(angles)
    lane, row = iota((8, 128), 1), iota((8, 128), 0)

    def pack(q, carry):
        at = pl.multiple_of(q * 16, 16)
        zero = views[0, pl.ds(at, 16), :].astype(F32)
        one = views[1, pl.ds(at, 16), :].astype(F32)
        for i in range(4):
            both = jnp.concatenate([zero[4 * i : 4 * i + 4], one[4 * i : 4 * i + 4]], axis=0)
            ends = every_lane(both[:, :128], 127), every_lane(both[:, 1152:], 0)
            line = jnp.where(lane == row + 8, ends[0], table)
            line = jnp.where(lane == row + 16, ends[1], line)
            send_extra[4 * q + i] = jnp.sum(line, axis=0, keepdims=True)
            send[4 * q + i] = jnp.concatenate([both[:, 128:640], both[:, 640:1152]], axis=0).astype(
                BF16
            )
        return carry

    lax.fori_loop(0, GROUP // 4, pack, 0)
    recv[me] = send[me]
    recv_extra[me] = send_extra[me]
    own[...] = jnp.zeros_like(own)
    first_cat[...] = build_first(w_first[...], b_first[...])
    second_cat[...], second_t[...] = build_second(w_second[...])
    gather_first[...], gather_second[...] = build_gather()
    pl.semaphore_wait(pltpu.get_barrier_semaphore(), GROUP - 1 + 2 * SUBS - 1)

    def remote(src, dst, send_sem, recv_sem, target):
        return pltpu.make_async_remote_copy(
            src_ref=src,
            dst_ref=dst,
            send_sem=send_sem,
            recv_sem=recv_sem,
            device_id=target,
            device_id_type=MESH,
        )

    def data_copy(other, slot):
        return remote(
            send.at[other], recv.at[slot], data_send.at[other], data_recv.at[slot], ring(other)
        )

    def extra_copy(other, slot):
        return remote(
            send_extra.at[other],
            recv_extra.at[slot],
            extra_send.at[other],
            extra_recv.at[slot],
            ring(other),
        )

    for p in range(1, GROUP):
        extra_copy(group_target(p), me).start()
        data_copy(group_target(p), me).start()

    def two_senders(p, carry):
        for q in range(2):
            other = group_source(2 * p + q)

            def arrived(other=other):
                extra_copy(other, other).wait_recv()
                data_copy(other, other).wait_recv()

            if q == 0:
                pl.when(p > 0)(arrived)
            else:
                arrived()
        for q in range(2):
            other = group_source(2 * p + q)
            add_sender(recv[other], recv_extra[other], windows.at[q], own)
        return carry

    lax.fori_loop(0, GROUP // 2, two_senders, 0)
    own[...] = own[...] * (math.pi / VPS)

    to_after = remote(
        own.at[2:4], field.at[0:2], halo_send.at[0], halo_recv.at[0], ring(lax.rem(me + 1, GROUP))
    )
    to_before = remote(
        own.at[0:2], field.at[6:8], halo_send.at[1], halo_recv.at[1], ring(lax.rem(me + GROUP - 1, GROUP))
    )

    def eighth(index):
        return pl.ds(pl.multiple_of(index * 128, 128), 128)

    def part_copy(p, arriving):
        other, target = sub_peer(p)
        slot = other if arriving else sub
        return remote(
            own.at[:, :, eighth(other)],
            eighths.at[slot],
            part_send.at[other],
            part_recv.at[slot],
            target,
        )

    def total_copy(p, arriving):
        other, target = sub_peer(p)
        slot = other if arriving else sub
        return remote(
            piece, totals.at[:, :, eighth(slot)], tot_send.at[other], tot_recv.at[slot], target
        )

    def slab_copy(p, arriving):
        other, target = slab_peer(p)
        slot = other if arriving else slab
        return remote(
            mine.at[0], part_slots.at[slot], slab_send.at[other], slab_recv.at[slot], target
        )

    def pair_copy(p, arriving):
        other, target = pair_peer(p)
        slot = other if arriving else pair
        return remote(
            mine.at[1], whole_slots.at[slot], pair_send.at[other], pair_recv.at[slot], target
        )

    def started(make, count):
        for p in range(count - 1):
            make(p, False).start()

    def finished(make, count):
        for p in range(count - 1):
            make(p, True).wait()

    started(part_copy, SUBS)
    to_after.start()
    to_before.start()
    eighths[sub] = own[:, :, eighth(sub)]
    taps[...] = jnp.zeros_like(taps)
    near_r[...] = jnp.zeros_like(near_r)
    acc_first[...] = jnp.zeros_like(acc_first)
    acc_second[...] = jnp.zeros_like(acc_second)
    ones = (iota((8, X), 0) == 0).astype(F32)

    def place(m, value):
        near_u[m] = jnp.concatenate([shifted(value, 1), value, shifted(value, -1)], axis=0)

    def forward(j, carry):
        patch = jnp.concatenate([near_u[j], near_u[j + 1], near_u[j + 2], ones], axis=0)
        high, low = split(patch)
        patch_u[j] = high
        pre = jnp.dot(
            first_cat[...], jnp.concatenate([high, high, low], axis=0), preferred_element_type=F32
        )
        outside = ((j == 0) & (me == 0)) | ((j == 5) & (me == GROUP - 1))
        hidden = jnp.maximum(pre, 0.0) * jnp.where(outside, 0.0, 1.0)
        high, low = split(hidden)
        hidden_all[j] = high
        main = jnp.dot(second_t[...], high, preferred_element_type=F32)
        rest = jnp.dot(second_t[0:PATCH], low, preferred_element_type=F32)
        added = main[:72] + (main[PATCH : PATCH + 72] + rest[:72])
        for shift_z in range(3):
            at = j - shift_z + 2
            taps[at] = taps[at] + added[24 * shift_z : 24 * shift_z + 24]
        return carry

    for i in range(DEPTH):
        place(i + 2, own[i])
    lax.fori_loop(2, 4, forward, 0)
    finished(part_copy, SUBS)
    total = eighths[0]
    for s in range(1, SUBS):
        total = total + eighths[s]
    piece[...] = total
    totals[:, :, eighth(sub)] = total
    started(total_copy, SUBS)
    to_after.wait()
    to_before.wait()
    for m in range(2):
        place(m, jnp.where(me > 0, field[m], 0.0))
        place(m + 6, jnp.where(me < GROUP - 1, field[m + 6], 0.0))
    lax.fori_loop(0, 2, forward, 0)
    lax.fori_loop(4, 6, forward, 0)
    finished(total_copy, SUBS)

    sum_square = jnp.zeros((8, X), F32)
    sum_resid = jnp.zeros((8, X), F32)
    for i in range(DEPTH):
        value = own[i]
        conv = shifted(taps[i + 2, 0:8], 1) + taps[i + 2, 8:16] + shifted(taps[i + 2, 16:24], -1)
        pred = value + conv + b_second[0]
        target = (totals[i] - value) / (SUBS - 1)
        pred_out[i] = pred
        target_out[i] = target
        diff = pred - target
        resid = (2.0 * diff) / CELLS
        sum_square = sum_square + diff * diff
        sum_resid = sum_resid + resid
        near_r[i + 2] = jnp.concatenate([shifted(resid, -1), resid, shifted(resid, 1)], axis=0)

    nothing = jnp.zeros((8, X), F32)

    def backward(j, carry):
        patch = jnp.concatenate([near_r[j + 2], near_r[j + 1], near_r[j], nothing], axis=0)
        high, low = split(patch)
        grad = jnp.dot(
            second_cat[...], jnp.concatenate([high, high, low], axis=0), preferred_element_type=F32
        )
        hidden = hidden_all[j]
        acc_second[:, :PATCH] += dot_nt(hidden, high)
        grad = jnp.where(hidden.astype(F32) > 0.0, grad, 0.0).astype(BF16)
        acc_first[:, :PATCH] += dot_nt(grad, patch_u[j])
        return carry

    lax.fori_loop(0, 6, backward, 0, unroll=2)

    packed = gathered(acc_first[...], gather_first[...])
    packed = packed + gathered(acc_second[...], gather_second[...])
    packed = packed[:16] + pltpu.roll(packed[16:], 64, 1)
    row, lane = iota((16, 128), 0), iota((16, 128), 1)
    packed = packed + jnp.where((row == 0) & (lane == 60), jnp.sum(sum_square) / CELLS, 0.0)
    packed = packed + jnp.where((row == 0) & (lane == 61), jnp.sum(sum_resid), 0.0)

    mine[0] = packed
    part_slots[slab] = packed
    started(slab_copy, SLABS)
    finished(slab_copy, SLABS)
    packed = part_slots[0]
    for s in range(1, 16):
        packed = packed + part_slots[s]
    mine[1] = packed
    whole_slots[pair] = packed
    started(pair_copy, 2 * SUBS)
    finished(pair_copy, 2 * SUBS)
    packed = whole_slots[0]
    for s in range(1, 16):
        packed = packed + whole_slots[s]
    grads_out[...] = packed

    def sent(p, carry):
        other = lax.rem(me + p, GROUP)
        extra_copy(other, me).wait_send()
        data_copy(other, me).wait_send()
        return carry

    lax.fori_loop(1, GROUP, sent, 0)


def finish_kernel(pred, target, packed, pred_out, target_out, loss, g_w1, g_b1, g_w2, g_b2, sems):
    copies = [
        pltpu.make_async_copy(pred, pred_out, sems.at[0]),
        pltpu.make_async_copy(target, target_out, sems.at[1]),
    ]
    for copy in copies:
        copy.start()
    value = packed[...]
    both = jnp.concatenate([value, pltpu.roll(value, 64, 1)], axis=0)
    g_w1[...] = both[:, :27]
    g_w2[...] = both[:, 32:59]
    row, lane = iota((CH, 128), 0), iota((CH, 128), 1)
    column = jnp.sum(jnp.where(lane == 27, both, 0.0), axis=1, keepdims=True)
    g_b1[...] = jnp.sum(jnp.where(lane == row, column, 0.0), axis=0, keepdims=True)[:, :CH]
    loss[...] = value[0:1, 60:61]
    g_b2[...] = value[0:1, 61:62]
    for copy in copies:
        copy.wait()


VMEM = pl.BlockSpec(memory_space=pltpu.VMEM)
SMEM = pl.BlockSpec(memory_space=pltpu.SMEM)
ANY = pl.BlockSpec(memory_space=pl.ANY)
HBM = pl.BlockSpec(memory_space=pltpu.HBM)


def shape(dims, dtype=F32):
    return jax.ShapeDtypeStruct(dims, dtype)


def body(sinogram, angles, w_first, b_first, w_second, b_second):
    dma = pltpu.SemaphoreType.DMA
    vmem = pltpu.VMEM
    pred, target, grads = pl.pallas_call(
        step_kernel,
        name="train_step",
        out_shape=(shape((DEPTH, Y, X)), shape((DEPTH, Y, X)), shape((16, 128))),
        in_specs=[HBM, SMEM] + [VMEM] * 3 + [SMEM],
        out_specs=[VMEM] * 3,
        scratch_shapes=[
            vmem((2, 128, COLS), BF16),
            vmem((GROUP, 16, X // 2), BF16),
            vmem((GROUP, 16, X // 2), BF16),
            vmem((GROUP, 1, 128), F32),
            vmem((GROUP, 1, 128), F32),
            vmem((2, X // 128, 8, 384), F32),
            vmem((DEPTH, Y, X), F32),
            vmem((256, 3 * PATCH), BF16),
            vmem((256, 3 * PATCH), BF16),
            vmem((2 * PATCH, 256), BF16),
            vmem((1024, 128), BF16),
            vmem((1024, 128), BF16),
            vmem((8, Y, X), F32),
            vmem((SUBS, DEPTH, Y, 128), F32),
            vmem((DEPTH, Y, 128), F32),
            vmem((DEPTH, Y, X), F32),
            vmem((8, 24, X), F32),
            vmem((6, PATCH, X), BF16),
            vmem((6, 256, X), BF16),
            vmem((8, 24, X), F32),
            vmem((8, 24, X), F32),
            vmem((256, 128), F32),
            vmem((256, 128), F32),
            vmem((16, 16, 128), F32),
            vmem((16, 16, 128), F32),
            vmem((2, 16, 128), F32),
            dma((1,)),
            dma((GROUP,)),
            dma((GROUP,)),
            dma((GROUP,)),
            dma((GROUP,)),
            dma((2,)),
            dma((2,)),
        ]
        + [dma((SUBS,))] * 4
        + [dma((16,))] * 4,
        compiler_params=pltpu.CompilerParams(
            collective_id=0, has_side_effects=True, vmem_limit_bytes=62 << 20
        ),
    )(sinogram, angles, w_first, b_first[None], w_second, b_second)
    pred, target, loss, g_w1, g_b1, g_w2, g_b2 = pl.pallas_call(
        finish_kernel,
        name="finish",
        out_shape=(
            shape((1, DEPTH, Y, X)),
            shape((1, DEPTH, Y, X)),
            shape((1, 1)),
            shape((CH, 27)),
            shape((1, CH)),
            shape((CH, 27)),
            shape((1, 1)),
        ),
        in_specs=[VMEM] * 3,
        out_specs=[ANY] * 2 + [VMEM] * 5,
        scratch_shapes=[dma((2,))],
        compiler_params=pltpu.CompilerParams(vmem_limit_bytes=62 << 20),
    )(pred[None], target[None], grads)
    return pred, target, loss.reshape(()), g_w1, g_b1.reshape(CH), g_w2, g_b2.reshape(1)


def solution(mesh):
    finer = Mesh(mesh.devices.reshape(SUBS, 2, SLABS), ("sub", "half", "slab"))
    every = ("sub", "half", "slab")
    return jax.shard_map(
        body,
        mesh=finer,
        in_specs=(P(every, None, None), P(every), P(), P(), P(), P()),
        out_specs=(
            P(("sub", "half"), "slab", None, None),
            P(("sub", "half"), "slab", None, None),
            P(),
            P(),
            P(),
            P(),
            P(),
        ),
        check_vma=False,
    )
```

```python
import math

import jax
import jax.numpy as jnp
from jax import lax
from jax.experimental import pallas as pl
from jax.experimental.pallas import tpu as pltpu
from jax.sharding import Mesh
from jax.sharding import PartitionSpec as P

DET = 2048
X = 1024
Y = 8
CH = 32
DEPTH = 4
SUBS = 8
SLABS = 16
GROUP = 2 * SLABS
VPS = 64
FIRST_COL = 384
COLS = 1280
PATCH = 80
CELLS = float(SUBS * 128 * Y * X)
MESH = pl.DeviceIdType.MESH
F32 = jnp.float32
BF16 = jnp.bfloat16

GATHER = lax.GatherDimensionNumbers(
    offset_dims=(),
    collapsed_slice_dims=(1,),
    start_index_map=(1,),
    operand_batching_dims=(0,),
    start_indices_batching_dims=(0,),
)


def iota(shape, dim):
    return lax.broadcasted_iota(jnp.int32, shape, dim)


def exact_dot(a, b):
    return jnp.dot(a, b, precision=lax.Precision.HIGHEST, preferred_element_type=F32)


def dot_nt(a, b, precision=None):
    return lax.dot_general(
        a, b, (((1,), (1,)), ((), ())), precision=precision, preferred_element_type=F32
    )


def split(value):
    high = value.astype(BF16)
    return high, (value - high.astype(F32)).astype(BF16)


def tap_of(block, shift_y):
    shift_z = (block >= 3).astype(jnp.int32) + (block >= 6).astype(jnp.int32)
    return 6 * shift_z + block + 3 * shift_y


def build_first(w_first, b_first):
    pick = (iota((256, CH), 0) & (CH - 1) == iota((256, CH), 1)).astype(F32)
    rows = exact_dot(pick, w_first)
    bias = jnp.sum(pick * b_first, axis=1, keepdims=True)
    row, col = iota((256, PATCH), 0), iota((256, PATCH), 1)
    out = jnp.where(col == 72, bias, 0.0)
    tap, at = iota((27, PATCH), 0), iota((27, PATCH), 1)
    for shift_y in range(3):
        expand = ((tap == tap_of(at >> 3, shift_y)) & (at < 72)).astype(F32)
        near = (col & 7) - (row >> 5) == shift_y - 1
        out = out + jnp.where(near & (col < 72), exact_dot(rows, expand), 0.0)
    high, low = split(out)
    return jnp.concatenate([high, low, high], axis=1)


def build_second(w_second):
    pick = (iota((256, CH), 0) & (CH - 1) == iota((256, CH), 1)).astype(F32)
    rows = exact_dot(pick, w_second)
    row, col = iota((256, PATCH), 0), iota((256, PATCH), 1)
    pick_t = (iota((CH, 256), 1) & (CH - 1) == iota((CH, 256), 0)).astype(F32)
    row_t, col_t = iota((PATCH, 256), 0), iota((PATCH, 256), 1)
    out = jnp.zeros((256, PATCH), F32)
    out_t = jnp.zeros((PATCH, 256), F32)
    tap, at = iota((27, PATCH), 0), iota((27, PATCH), 1)
    tap_t, at_t = iota((PATCH, 27), 1), iota((PATCH, 27), 0)
    for shift_y in range(3):
        expand = ((tap == tap_of(at >> 3, shift_y)) & (at < 72)).astype(F32)
        near = (row >> 5) - (col & 7) == shift_y - 1
        out = out + jnp.where(near & (col < 72), exact_dot(rows, expand), 0.0)
        expand_t = ((tap_t == tap_of(at_t >> 3, shift_y)) & (at_t < 72)).astype(F32)
        taps_t = dot_nt(expand_t, w_second, lax.Precision.HIGHEST)
        near_t = (col_t >> 5) - (row_t & 7) == shift_y - 1
        out_t = out_t + jnp.where(near_t & (row_t < 72), exact_dot(taps_t, pick_t), 0.0)
    high, low = split(out)
    return jnp.concatenate([high, low, high], axis=1), jnp.concatenate(split(out_t), axis=0)


def build_gather():
    row, lane = iota((1024, 128), 0), iota((1024, 128), 1)
    y, col = row >> 7, row & 127
    block, near = col >> 3, col & 7
    shift = near - y + 1
    inside = (col < 72) & (shift >= 0) & (shift <= 2)
    first = (inside & (lane == tap_of(block, shift))) | ((col == 72) & (lane == 27))
    shift = y - near + 1
    inside = (col < 72) & (shift >= 0) & (shift <= 2)
    second = inside & (lane == tap_of(block, shift) + 32)
    return first.astype(F32).astype(BF16), second.astype(F32).astype(BF16)


def gathered(sums, gather):
    wide = jnp.concatenate([sums[CH * y : CH * y + CH] for y in range(Y)], axis=1)
    high, rest = wide.astype(BF16), wide
    rest = wide - high.astype(F32)
    middle, low = split(rest)
    out = jnp.dot(
        jnp.concatenate([high, middle, low], axis=0), gather, preferred_element_type=F32
    )
    return out[:CH] + (out[CH : 2 * CH] + out[2 * CH :])


def shifted(value, by):
    lane = iota(value.shape, 1)
    if by == 1:
        return jnp.where(lane == 0, 0.0, pltpu.roll(value, 1, 1))
    return jnp.where(lane == X - 1, 0.0, pltpu.roll(value, X - 1, 1))


def take(source, index):
    return lax.gather(
        source, index[..., None], GATHER, (1, 1), mode=lax.GatherScatterMode.PROMISE_IN_BOUNDS
    )


def view_table(angles):
    lane, row = iota((8, 128), 1), iota((8, 128), 0)
    angle = jnp.where(lane < 2, angles[0], angles[1])
    value = jnp.where(lane & 1 == 0, jnp.cos(angle), jnp.sin(angle))
    return jnp.where((row == 0) & (lane < 4), value, 0.0)


def every_lane(source, index):
    return take(source, jnp.full((8, 128), index, jnp.int32))


def window_range(part_x):
    ends = (abs(128 * part_x - 511.5), abs(128 * part_x - 384.5))
    middle = (DET - 1) / 2.0
    first = (math.floor(middle - max(ends) - 4.0) - FIRST_COL) // 64
    last = (math.floor(middle + min(ends) + 0.5) - FIRST_COL) // 64
    return first, last


def add_sender(block, extra, windows, out):
    value = block.astype(F32)
    tables = jnp.broadcast_to(extra, (8, 128))
    ends = [take(tables, iota((8, 128), 0) + at) for at in (8, 16)]
    row = jnp.concatenate([ends[0], value[:8], value[8:], ends[1]], axis=1)
    moved = pltpu.roll(row, COLS - 64, 1)
    views = [every_lane(tables, i) for i in range(4)]
    row_index = iota((8, 128), 0)
    row_pos = row_index.astype(F32) - (Y - 1) / 2.0
    lane = iota((8, 128), 1).astype(F32)

    def piece(k):
        source = moved if k & 1 else row
        return source[:, (k >> 1) * 128 : (k >> 1) * 128 + 128]

    lowest = []
    for part_x in range(X // 128):
        begin = 128.0 * part_x - (X - 1) / 2.0
        both = []
        for v in range(2):
            cosine, sine = views[2 * v], views[2 * v + 1]
            least = jnp.minimum(begin * cosine, (begin + 127.0) * cosine)
            both.append(jnp.floor((least - 3.5 * jnp.abs(sine)) + (DET - 1) / 2.0))
        lowest.append(both)
        offset = jnp.where(row_index < 4, both[0], both[1]) - float(FIRST_COL)
        step = jnp.floor(offset * (1.0 / 64.0))
        first, last = window_range(part_x)
        near, far = piece(first), piece(first + 2)
        for k in range(first + 1, last + 1):
            reached = step >= float(k)
            near = jnp.where(reached, piece(k), near)
            far = jnp.where(reached, piece(k + 2), far)
        moved_by = (offset - 64.0 * step).astype(jnp.int32)
        place = moved_by + iota((8, 128), 1)
        at = place & 127
        window = [
            jnp.where(place < 128, take(near, at), take(far, at)),
            take(far, moved_by),
            take(far, moved_by + 1),
        ]
        windows[part_x] = jnp.concatenate(window, axis=1)
    for part_x in range(X // 128):
        here = slice(part_x * 128, (part_x + 1) * 128)
        total = [out[z, :, here] for z in range(DEPTH)]
        for v in range(2):
            cosine, sine = views[2 * v], views[2 * v + 1]
            pos = (
                (lane + (128.0 * part_x - (X - 1) / 2.0)) * cosine + row_pos * sine
            ) + (DET - 1) / 2.0
            lower = jnp.floor(pos)
            part = pos - lower
            w_high = part.astype(BF16).astype(F32)
            w_low = (1.0 - part).astype(BF16).astype(F32)
            index = (lower - lowest[part_x][v]).astype(jnp.int32)
            index = jnp.concatenate([index, index], axis=0)
            at_low = (index & 127).astype(jnp.int16)
            at_high = ((index + 1) & 127).astype(jnp.int16)
            whole = index.astype(jnp.int16)
            in_low = whole < jnp.int16(128)
            in_high = whole < jnp.int16(127)
            for pair in range(2):

                def source(offset):
                    first_row = v * 4 + 2 * pair
                    parts = [
                        jnp.broadcast_to(
                            windows[part_x, pl.ds(first_row + q, 1), pl.ds(offset, 128)], (8, 128)
                        )
                        for q in range(2)
                    ]
                    return jnp.concatenate(parts, axis=0).astype(BF16)

                near, next_one, after = source(0), source(128), source(256)
                low = jnp.where(in_low, take(near, at_low), next_one).astype(F32)
                high = jnp.where(in_low, next_one, after)
                high = jnp.where(in_high, take(near, at_high), high).astype(F32)
                for q in range(2):
                    z = 2 * pair + q
                    half = slice(8 * q, 8 * q + 8)
                    total[z] = total[z] + (w_low * low[half] + w_high * high[half])
        for z in range(DEPTH):
            out[z, :, here] = total[z]


def step_kernel(
    sino,
    angles,
    w_first,
    b_first,
    w_second,
    b_second,
    pred_out,
    target_out,
    grads_out,
    views,
    send,
    recv,
    send_extra,
    recv_extra,
    windows,
    own,
    first_cat,
    second_cat,
    second_t,
    gather_first,
    gather_second,
    field,
    eighths,
    piece,
    totals,
    near_u,
    patch_u,
    hidden_all,
    taps,
    near_r,
    acc_first,
    acc_second,
    part_slots,
    whole_slots,
    mine,
    local_sem,
    data_send,
    data_recv,
    extra_send,
    extra_recv,
    halo_send,
    halo_recv,
    part_send,
    part_recv,
    tot_send,
    tot_recv,
    slab_send,
    slab_recv,
    pair_send,
    pair_recv,
):
    sub, half, slab = lax.axis_index("sub"), lax.axis_index("half"), lax.axis_index("slab")
    me = half * SLABS + slab
    pair = sub * 2 + half

    def ring(other):
        return (sub, other >> 4, other & 15)

    far_first = (2, 1, 3, 0)

    def slab_peer(p):
        y = ((slab >> 2) + far_first[p >> 2]) & 3
        other = y * 4 + ((slab + far_first[p & 3]) & 3)
        return other, (sub, half, other)

    def sub_at(p):
        x = ((sub >> 1) + far_first[p >> 1]) & 3
        return x * 2 + ((sub + 1 + p) & 1)

    def pair_peer(p):
        other_sub, other_half = sub_at(p >> 1), (half + 1 + p) & 1
        return other_sub * 2 + other_half, (other_sub, other_half, slab)

    def sub_peer(p):
        other = sub_at(p)
        return other, (other, half, slab)

    def distance(p):
        if p < 8:
            return p & 1, p >> 1, 0
        q = p - 8
        return (q // 3) & 1, q // 6, far_first[q % 3]

    def group_target(p):
        core, y, z = distance(p)
        return ((half + core) & 1) * SLABS + (((slab >> 2) + y) & 3) * 4 + ((slab + z) & 3)

    def group_source(p):
        q = p - 8
        third = lax.rem(q, 3)
        near = p < 8
        core = jnp.where(near, p, q // 3) & 1
        y = jnp.where(near, p >> 1, q // 6)
        z = jnp.where(near, 0, jnp.where(third == 0, 2, jnp.where(third == 1, 1, 3)))
        row = ((slab >> 2) + 4 - y) & 3
        return ((half + core) & 1) * SLABS + row * 4 + ((slab + 4 - z) & 3)

    def group_peer(p):
        other = group_target(GROUP - 1 - p)
        return other, ring(other)

    def greet(peer, count):
        for p in range(count - 1):
            pl.semaphore_signal(
                pltpu.get_barrier_semaphore(), inc=1, device_id=peer(p)[1], device_id_type=MESH
            )

    load = pltpu.make_async_copy(
        sino.at[:, :, pl.ds(FIRST_COL, COLS)], views, local_sem.at[0]
    )
    load.start()
    greet(group_peer, GROUP)
    greet(pair_peer, 2 * SUBS)
    load.wait()

    table = view_table(angles)
    lane, row = iota((8, 128), 1), iota((8, 128), 0)

    def pack(q, carry):
        at = pl.multiple_of(q * 16, 16)
        zero = views[0, pl.ds(at, 16), :].astype(F32)
        one = views[1, pl.ds(at, 16), :].astype(F32)
        for i in range(4):
            both = jnp.concatenate([zero[4 * i : 4 * i + 4], one[4 * i : 4 * i + 4]], axis=0)
            ends = every_lane(both[:, :128], 127), every_lane(both[:, 1152:], 0)
            line = jnp.where(lane == row + 8, ends[0], table)
            line = jnp.where(lane == row + 16, ends[1], line)
            send_extra[4 * q + i] = jnp.sum(line, axis=0, keepdims=True)
            send[4 * q + i] = jnp.concatenate([both[:, 128:640], both[:, 640:1152]], axis=0).astype(
                BF16
            )
        return carry

    lax.fori_loop(0, GROUP // 4, pack, 0)
    recv[me] = send[me]
    recv_extra[me] = send_extra[me]
    own[...] = jnp.zeros_like(own)
    pl.semaphore_wait(pltpu.get_barrier_semaphore(), GROUP - 1 + 2 * SUBS - 1)

    def remote(src, dst, send_sem, recv_sem, target):
        return pltpu.make_async_remote_copy(
            src_ref=src,
            dst_ref=dst,
            send_sem=send_sem,
            recv_sem=recv_sem,
            device_id=target,
            device_id_type=MESH,
        )

    def data_copy(other, slot):
        return remote(
            send.at[other], recv.at[slot], data_send.at[other], data_recv.at[slot], ring(other)
        )

    def extra_copy(other, slot):
        return remote(
            send_extra.at[other],
            recv_extra.at[slot],
            extra_send.at[other],
            extra_recv.at[slot],
            ring(other),
        )

    for p in range(1, GROUP):
        extra_copy(group_target(p), me).start()
        data_copy(group_target(p), me).start()

    first_cat[...] = build_first(w_first[...], b_first[...])
    second_cat[...], second_t[...] = build_second(w_second[...])

    def two_senders(p, carry):
        for q in range(2):
            other = group_source(2 * p + q)

            def arrived(other=other):
                extra_copy(other, other).wait_recv()
                data_copy(other, other).wait_recv()

            if q == 0:
                pl.when(p > 0)(arrived)
            else:
                arrived()
        for q in range(2):
            other = group_source(2 * p + q)
            add_sender(recv[other], recv_extra[other], windows.at[q], own)
        return carry

    lax.fori_loop(0, GROUP // 2, two_senders, 0)
    own[...] = own[...] * (math.pi / VPS)

    to_after = remote(
        own.at[2:4], field.at[0:2], halo_send.at[0], halo_recv.at[0], ring(lax.rem(me + 1, GROUP))
    )
    to_before = remote(
        own.at[0:2], field.at[6:8], halo_send.at[1], halo_recv.at[1], ring(lax.rem(me + GROUP - 1, GROUP))
    )

    def eighth(index):
        return pl.ds(pl.multiple_of(index * 128, 128), 128)

    def part_copy(p, arriving):
        other, target = sub_peer(p)
        slot = other if arriving else sub
        return remote(
            own.at[:, :, eighth(other)],
            eighths.at[slot],
            part_send.at[other],
            part_recv.at[slot],
            target,
        )

    def total_copy(p, arriving):
        other, target = sub_peer(p)
        slot = other if arriving else sub
        return remote(
            piece, totals.at[:, :, eighth(slot)], tot_send.at[other], tot_recv.at[slot], target
        )

    def slab_copy(p, arriving):
        other, target = slab_peer(p)
        slot = other if arriving else slab
        return remote(
            mine.at[0], part_slots.at[slot], slab_send.at[other], slab_recv.at[slot], target
        )

    def pair_copy(p, arriving):
        other, target = pair_peer(p)
        slot = other if arriving else pair
        return remote(
            mine.at[1], whole_slots.at[slot], pair_send.at[other], pair_recv.at[slot], target
        )

    def started(make, count):
        for p in range(count - 1):
            make(p, False).start()

    def finished(make, count):
        for p in range(count - 1):
            make(p, True).wait()

    started(part_copy, SUBS)
    to_after.start()
    to_before.start()
    eighths[sub] = own[:, :, eighth(sub)]
    taps[...] = jnp.zeros_like(taps)
    near_r[...] = jnp.zeros_like(near_r)
    acc_first[...] = jnp.zeros_like(acc_first)
    acc_second[...] = jnp.zeros_like(acc_second)
    ones = (iota((8, X), 0) == 0).astype(F32)

    def place(m, value):
        near_u[m] = jnp.concatenate([shifted(value, 1), value, shifted(value, -1)], axis=0)

    def forward(j, carry):
        patch = jnp.concatenate([near_u[j], near_u[j + 1], near_u[j + 2], ones], axis=0)
        high, low = split(patch)
        patch_u[j] = high
        pre = jnp.dot(
            first_cat[...], jnp.concatenate([high, high, low], axis=0), preferred_element_type=F32
        )
        outside = ((j == 0) & (me == 0)) | ((j == 5) & (me == GROUP - 1))
        hidden = jnp.maximum(pre, 0.0) * jnp.where(outside, 0.0, 1.0)
        high, low = split(hidden)
        hidden_all[j] = high
        main = jnp.dot(second_t[...], high, preferred_element_type=F32)
        rest = jnp.dot(second_t[0:PATCH], low, preferred_element_type=F32)
        added = main[:72] + (main[PATCH : PATCH + 72] + rest[:72])
        for shift_z in range(3):
            at = j - shift_z + 2
            taps[at] = taps[at] + added[24 * shift_z : 24 * shift_z + 24]
        return carry

    for i in range(DEPTH):
        place(i + 2, own[i])
    lax.fori_loop(2, 4, forward, 0)
    gather_first[...], gather_second[...] = build_gather()
    finished(part_copy, SUBS)
    total = eighths[0]
    for s in range(1, SUBS):
        total = total + eighths[s]
    piece[...] = total
    totals[:, :, eighth(sub)] = total
    started(total_copy, SUBS)
    to_after.wait()
    to_before.wait()
    for m in range(2):
        place(m, jnp.where(me > 0, field[m], 0.0))
        place(m + 6, jnp.where(me < GROUP - 1, field[m + 6], 0.0))
    lax.fori_loop(0, 2, forward, 0)
    lax.fori_loop(4, 6, forward, 0)
    finished(total_copy, SUBS)

    sum_square = jnp.zeros((8, X), F32)
    sum_resid = jnp.zeros((8, X), F32)
    for i in range(DEPTH):
        value = own[i]
        conv = shifted(taps[i + 2, 0:8], 1) + taps[i + 2, 8:16] + shifted(taps[i + 2, 16:24], -1)
        pred = value + conv + b_second[0]
        target = (totals[i] - value) / (SUBS - 1)
        pred_out[i] = pred
        target_out[i] = target
        diff = pred - target
        resid = (2.0 * diff) / CELLS
        sum_square = sum_square + diff * diff
        sum_resid = sum_resid + resid
        near_r[i + 2] = jnp.concatenate([shifted(resid, -1), resid, shifted(resid, 1)], axis=0)

    nothing = jnp.zeros((8, X), F32)

    def backward(j, carry):
        patch = jnp.concatenate([near_r[j + 2], near_r[j + 1], near_r[j], nothing], axis=0)
        high, low = split(patch)
        grad = jnp.dot(
            second_cat[...], jnp.concatenate([high, high, low], axis=0), preferred_element_type=F32
        )
        hidden = hidden_all[j]
        acc_second[:, :PATCH] += dot_nt(hidden, high)
        grad = jnp.where(hidden.astype(F32) > 0.0, grad, 0.0).astype(BF16)
        acc_first[:, :PATCH] += dot_nt(grad, patch_u[j])
        return carry

    lax.fori_loop(0, 6, backward, 0, unroll=3)

    packed = gathered(acc_first[...], gather_first[...])
    packed = packed + gathered(acc_second[...], gather_second[...])
    packed = packed[:16] + pltpu.roll(packed[16:], 64, 1)
    row, lane = iota((16, 128), 0), iota((16, 128), 1)
    packed = packed + jnp.where((row == 0) & (lane == 60), jnp.sum(sum_square) / CELLS, 0.0)
    packed = packed + jnp.where((row == 0) & (lane == 61), jnp.sum(sum_resid), 0.0)

    mine[1] = packed
    whole_slots[pair] = packed
    started(pair_copy, 2 * SUBS)
    finished(pair_copy, 2 * SUBS)
    packed = whole_slots[0]
    for s in range(1, 16):
        packed = packed + whole_slots[s]
    mine[0] = packed
    part_slots[slab] = packed
    started(slab_copy, SLABS)
    finished(slab_copy, SLABS)
    packed = part_slots[0]
    for s in range(1, 16):
        packed = packed + part_slots[s]
    grads_out[...] = packed

    def sent(p, carry):
        other = lax.rem(me + p, GROUP)
        extra_copy(other, me).wait_send()
        data_copy(other, me).wait_send()
        return carry

    lax.fori_loop(1, GROUP, sent, 0)


def finish_kernel(pred, target, packed, pred_out, target_out, loss, g_w1, g_b1, g_w2, g_b2, sems):
    copies = [
        pltpu.make_async_copy(pred, pred_out, sems.at[0]),
        pltpu.make_async_copy(target, target_out, sems.at[1]),
    ]
    for copy in copies:
        copy.start()
    value = packed[...]
    both = jnp.concatenate([value, pltpu.roll(value, 64, 1)], axis=0)
    g_w1[...] = both[:, :27]
    g_w2[...] = both[:, 32:59]
    row, lane = iota((CH, 128), 0), iota((CH, 128), 1)
    column = jnp.sum(jnp.where(lane == 27, both, 0.0), axis=1, keepdims=True)
    g_b1[...] = jnp.sum(jnp.where(lane == row, column, 0.0), axis=0, keepdims=True)[:, :CH]
    loss[...] = value[0:1, 60:61]
    g_b2[...] = value[0:1, 61:62]
    for copy in copies:
        copy.wait()


VMEM = pl.BlockSpec(memory_space=pltpu.VMEM)
SMEM = pl.BlockSpec(memory_space=pltpu.SMEM)
ANY = pl.BlockSpec(memory_space=pl.ANY)
HBM = pl.BlockSpec(memory_space=pltpu.HBM)


def shape(dims, dtype=F32):
    return jax.ShapeDtypeStruct(dims, dtype)


def body(sinogram, angles, w_first, b_first, w_second, b_second):
    dma = pltpu.SemaphoreType.DMA
    vmem = pltpu.VMEM
    pred, target, grads = pl.pallas_call(
        step_kernel,
        name="train_step",
        out_shape=(shape((DEPTH, Y, X)), shape((DEPTH, Y, X)), shape((16, 128))),
        in_specs=[HBM, SMEM] + [VMEM] * 3 + [SMEM],
        out_specs=[VMEM] * 3,
        scratch_shapes=[
            vmem((2, 128, COLS), BF16),
            vmem((GROUP, 16, X // 2), BF16),
            vmem((GROUP, 16, X // 2), BF16),
            vmem((GROUP, 1, 128), F32),
            vmem((GROUP, 1, 128), F32),
            vmem((2, X // 128, 8, 384), F32),
            vmem((DEPTH, Y, X), F32),
            vmem((256, 3 * PATCH), BF16),
            vmem((256, 3 * PATCH), BF16),
            vmem((2 * PATCH, 256), BF16),
            vmem((1024, 128), BF16),
            vmem((1024, 128), BF16),
            vmem((8, Y, X), F32),
            vmem((SUBS, DEPTH, Y, 128), F32),
            vmem((DEPTH, Y, 128), F32),
            vmem((DEPTH, Y, X), F32),
            vmem((8, 24, X), F32),
            vmem((6, PATCH, X), BF16),
            vmem((6, 256, X), BF16),
            vmem((8, 24, X), F32),
            vmem((8, 24, X), F32),
            vmem((256, 128), F32),
            vmem((256, 128), F32),
            vmem((16, 16, 128), F32),
            vmem((16, 16, 128), F32),
            vmem((2, 16, 128), F32),
            dma((1,)),
            dma((GROUP,)),
            dma((GROUP,)),
            dma((GROUP,)),
            dma((GROUP,)),
            dma((2,)),
            dma((2,)),
        ]
        + [dma((SUBS,))] * 4
        + [dma((16,))] * 4,
        compiler_params=pltpu.CompilerParams(
            collective_id=0, has_side_effects=True, vmem_limit_bytes=62 << 20
        ),
    )(sinogram, angles, w_first, b_first[None], w_second, b_second)
    pred, target, loss, g_w1, g_b1, g_w2, g_b2 = pl.pallas_call(
        finish_kernel,
        name="finish",
        out_shape=(
            shape((1, DEPTH, Y, X)),
            shape((1, DEPTH, Y, X)),
            shape((1, 1)),
            shape((CH, 27)),
            shape((1, CH)),
            shape((CH, 27)),
            shape((1, 1)),
        ),
        in_specs=[VMEM] * 3,
        out_specs=[ANY] * 2 + [VMEM] * 5,
        scratch_shapes=[dma((2,))],
        compiler_params=pltpu.CompilerParams(vmem_limit_bytes=62 << 20),
    )(pred[None], target[None], grads)
    return pred, target, loss.reshape(()), g_w1, g_b1.reshape(CH), g_w2, g_b2.reshape(1)


def solution(mesh):
    finer = Mesh(mesh.devices.reshape(SUBS, 2, SLABS), ("sub", "half", "slab"))
    every = ("sub", "half", "slab")
    return jax.shard_map(
        body,
        mesh=finer,
        in_specs=(P(every, None, None), P(every), P(), P(), P(), P()),
        out_specs=(
            P(("sub", "half"), "slab", None, None),
            P(("sub", "half"), "slab", None, None),
            P(),
            P(),
            P(),
            P(),
            P(),
        ),
        check_vma=False,
    )
```

```python
import math

import jax
import jax.numpy as jnp
from jax import lax
from jax.experimental import pallas as pl
from jax.experimental.pallas import tpu as pltpu
from jax.sharding import Mesh
from jax.sharding import PartitionSpec as P

DET = 2048
X = 1024
Y = 8
CH = 32
DEPTH = 4
SUBS = 8
SLABS = 16
GROUP = 2 * SLABS
VPS = 64
FIRST_COL = 384
COLS = 1280
PATCH = 80
CELLS = float(SUBS * 128 * Y * X)
MESH = pl.DeviceIdType.MESH
F32 = jnp.float32
BF16 = jnp.bfloat16

GATHER = lax.GatherDimensionNumbers(
    offset_dims=(),
    collapsed_slice_dims=(1,),
    start_index_map=(1,),
    operand_batching_dims=(0,),
    start_indices_batching_dims=(0,),
)


def iota(shape, dim):
    return lax.broadcasted_iota(jnp.int32, shape, dim)


def exact_dot(a, b):
    return jnp.dot(a, b, precision=lax.Precision.HIGHEST, preferred_element_type=F32)


def dot_nt(a, b, precision=None):
    return lax.dot_general(
        a, b, (((1,), (1,)), ((), ())), precision=precision, preferred_element_type=F32
    )


def split(value):
    high = value.astype(BF16)
    return high, (value - high.astype(F32)).astype(BF16)


def tap_of(block, shift_y):
    shift_z = (block >= 3).astype(jnp.int32) + (block >= 6).astype(jnp.int32)
    return 6 * shift_z + block + 3 * shift_y


def build_first(w_first, b_first):
    pick = (iota((256, CH), 0) & (CH - 1) == iota((256, CH), 1)).astype(F32)
    rows = exact_dot(pick, w_first)
    bias = jnp.sum(pick * b_first, axis=1, keepdims=True)
    row, col = iota((256, PATCH), 0), iota((256, PATCH), 1)
    out = jnp.where(col == 72, bias, 0.0)
    tap, at = iota((27, PATCH), 0), iota((27, PATCH), 1)
    for shift_y in range(3):
        expand = ((tap == tap_of(at >> 3, shift_y)) & (at < 72)).astype(F32)
        near = (col & 7) - (row >> 5) == shift_y - 1
        out = out + jnp.where(near & (col < 72), exact_dot(rows, expand), 0.0)
    high, low = split(out)
    return jnp.concatenate([high, low, high], axis=1)


def build_second(w_second):
    pick = (iota((256, CH), 0) & (CH - 1) == iota((256, CH), 1)).astype(F32)
    rows = exact_dot(pick, w_second)
    row, col = iota((256, PATCH), 0), iota((256, PATCH), 1)
    pick_t = (iota((CH, 256), 1) & (CH - 1) == iota((CH, 256), 0)).astype(F32)
    row_t, col_t = iota((PATCH, 256), 0), iota((PATCH, 256), 1)
    out = jnp.zeros((256, PATCH), F32)
    out_t = jnp.zeros((PATCH, 256), F32)
    tap, at = iota((27, PATCH), 0), iota((27, PATCH), 1)
    tap_t, at_t = iota((PATCH, 27), 1), iota((PATCH, 27), 0)
    for shift_y in range(3):
        expand = ((tap == tap_of(at >> 3, shift_y)) & (at < 72)).astype(F32)
        near = (row >> 5) - (col & 7) == shift_y - 1
        out = out + jnp.where(near & (col < 72), exact_dot(rows, expand), 0.0)
        expand_t = ((tap_t == tap_of(at_t >> 3, shift_y)) & (at_t < 72)).astype(F32)
        taps_t = dot_nt(expand_t, w_second, lax.Precision.HIGHEST)
        near_t = (col_t >> 5) - (row_t & 7) == shift_y - 1
        out_t = out_t + jnp.where(near_t & (row_t < 72), exact_dot(taps_t, pick_t), 0.0)
    high, low = split(out)
    return jnp.concatenate([high, low, high], axis=1), jnp.concatenate(split(out_t), axis=0)


def build_gather():
    row, lane = iota((1024, 128), 0), iota((1024, 128), 1)
    y, col = row >> 7, row & 127
    block, near = col >> 3, col & 7
    shift = near - y + 1
    inside = (col < 72) & (shift >= 0) & (shift <= 2)
    first = (inside & (lane == tap_of(block, shift))) | ((col == 72) & (lane == 27))
    shift = y - near + 1
    inside = (col < 72) & (shift >= 0) & (shift <= 2)
    second = inside & (lane == tap_of(block, shift) + 32)
    return first.astype(F32).astype(BF16), second.astype(F32).astype(BF16)


def gathered(sums, gather):
    wide = jnp.concatenate([sums[CH * y : CH * y + CH] for y in range(Y)], axis=1)
    high, rest = wide.astype(BF16), wide
    rest = wide - high.astype(F32)
    middle, low = split(rest)
    out = jnp.dot(
        jnp.concatenate([high, middle, low], axis=0), gather, preferred_element_type=F32
    )
    return out[:CH] + (out[CH : 2 * CH] + out[2 * CH :])


def shifted(value, by):
    lane = iota(value.shape, 1)
    if by == 1:
        return jnp.where(lane == 0, 0.0, pltpu.roll(value, 1, 1))
    return jnp.where(lane == X - 1, 0.0, pltpu.roll(value, X - 1, 1))


def take(source, index):
    return lax.gather(
        source, index[..., None], GATHER, (1, 1), mode=lax.GatherScatterMode.PROMISE_IN_BOUNDS
    )


def view_table(angles):
    lane, row = iota((8, 128), 1), iota((8, 128), 0)
    angle = jnp.where(lane < 2, angles[0], angles[1])
    value = jnp.where(lane & 1 == 0, jnp.cos(angle), jnp.sin(angle))
    return jnp.where((row == 0) & (lane < 4), value, 0.0)


def every_lane(source, index):
    return take(source, jnp.full((8, 128), index, jnp.int32))


def window_range(part_x):
    ends = (abs(128 * part_x - 511.5), abs(128 * part_x - 384.5))
    middle = (DET - 1) / 2.0
    first = (math.floor(middle - max(ends) - 4.0) - FIRST_COL) // 64
    last = (math.floor(middle + min(ends) + 0.5) - FIRST_COL) // 64
    return first, last


def add_sender(block, extra, windows, out):
    value = block.astype(F32)
    tables = jnp.broadcast_to(extra, (8, 128))
    ends = [take(tables, iota((8, 128), 0) + at) for at in (8, 16)]
    row = jnp.concatenate([ends[0], value[:8], value[8:], ends[1]], axis=1)
    moved = pltpu.roll(row, COLS - 64, 1)
    views = [every_lane(tables, i) for i in range(4)]
    row_index = iota((8, 128), 0)
    row_pos = row_index.astype(F32) - (Y - 1) / 2.0
    lane = iota((8, 128), 1).astype(F32)

    def piece(k):
        source = moved if k & 1 else row
        return source[:, (k >> 1) * 128 : (k >> 1) * 128 + 128]

    lowest = []
    for part_x in range(X // 128):
        begin = 128.0 * part_x - (X - 1) / 2.0
        both = []
        for v in range(2):
            cosine, sine = views[2 * v], views[2 * v + 1]
            least = jnp.minimum(begin * cosine, (begin + 127.0) * cosine)
            both.append(jnp.floor((least - 3.5 * jnp.abs(sine)) + (DET - 1) / 2.0))
        lowest.append(both)
        offset = jnp.where(row_index < 4, both[0], both[1]) - float(FIRST_COL)
        step = jnp.floor(offset * (1.0 / 64.0))
        first, last = window_range(part_x)
        near, far = piece(first), piece(first + 2)
        for k in range(first + 1, last + 1):
            reached = step >= float(k)
            near = jnp.where(reached, piece(k), near)
            far = jnp.where(reached, piece(k + 2), far)
        moved_by = (offset - 64.0 * step).astype(jnp.int32)
        place = moved_by + iota((8, 128), 1)
        at = place & 127
        window = [
            jnp.where(place < 128, take(near, at), take(far, at)),
            take(far, moved_by),
            take(far, moved_by + 1),
        ]
        windows[part_x] = jnp.concatenate(window, axis=1)
    for part_x in range(X // 128):
        here = slice(part_x * 128, (part_x + 1) * 128)
        total = [out[z, :, here] for z in range(DEPTH)]
        for v in range(2):
            cosine, sine = views[2 * v], views[2 * v + 1]
            pos = (
                (lane + (128.0 * part_x - (X - 1) / 2.0)) * cosine + row_pos * sine
            ) + (DET - 1) / 2.0
            lower = jnp.floor(pos)
            part = pos - lower
            w_high = part.astype(BF16).astype(F32)
            w_low = (1.0 - part).astype(BF16).astype(F32)
            index = (lower - lowest[part_x][v]).astype(jnp.int32)
            index = jnp.concatenate([index, index], axis=0)
            at_low = (index & 127).astype(jnp.int16)
            at_high = ((index + 1) & 127).astype(jnp.int16)
            whole = index.astype(jnp.int16)
            in_low = whole < jnp.int16(128)
            in_high = whole < jnp.int16(127)
            for pair in range(2):

                def source(offset):
                    first_row = v * 4 + 2 * pair
                    parts = [
                        jnp.broadcast_to(
                            windows[part_x, pl.ds(first_row + q, 1), pl.ds(offset, 128)], (8, 128)
                        )
                        for q in range(2)
                    ]
                    return jnp.concatenate(parts, axis=0).astype(BF16)

                near, next_one, after = source(0), source(128), source(256)
                low = jnp.where(in_low, take(near, at_low), next_one).astype(F32)
                high = jnp.where(in_low, next_one, after)
                high = jnp.where(in_high, take(near, at_high), high).astype(F32)
                for q in range(2):
                    z = 2 * pair + q
                    half = slice(8 * q, 8 * q + 8)
                    total[z] = total[z] + (w_low * low[half] + w_high * high[half])
        for z in range(DEPTH):
            out[z, :, here] = total[z]


def step_kernel(
    sino,
    angles,
    w_first,
    b_first,
    w_second,
    b_second,
    pred_out,
    target_out,
    grads_out,
    views,
    send,
    recv,
    send_extra,
    recv_extra,
    windows,
    own,
    first_cat,
    second_cat,
    second_t,
    gather_first,
    gather_second,
    field,
    eighths,
    piece,
    totals,
    near_u,
    patch_u,
    hidden_all,
    taps,
    near_r,
    acc_first,
    acc_second,
    part_slots,
    whole_slots,
    mine,
    local_sem,
    data_send,
    data_recv,
    extra_send,
    extra_recv,
    halo_send,
    halo_recv,
    part_send,
    part_recv,
    tot_send,
    tot_recv,
    slab_send,
    slab_recv,
    pair_send,
    pair_recv,
):
    sub, half, slab = lax.axis_index("sub"), lax.axis_index("half"), lax.axis_index("slab")
    me = half * SLABS + slab
    pair = sub * 2 + half

    def ring(other):
        return (sub, other >> 4, other & 15)

    far_first = (2, 1, 3, 0)

    def slab_peer(p):
        y = ((slab >> 2) + far_first[p >> 2]) & 3
        other = y * 4 + ((slab + far_first[p & 3]) & 3)
        return other, (sub, half, other)

    def sub_at(p):
        x = ((sub >> 1) + far_first[p >> 1]) & 3
        return x * 2 + ((sub + 1 + p) & 1)

    def pair_peer(p):
        other_sub, other_half = sub_at(p >> 1), (half + 1 + p) & 1
        return other_sub * 2 + other_half, (other_sub, other_half, slab)

    def sub_peer(p):
        other = sub_at(p)
        return other, (other, half, slab)

    def distance(p):
        if p < 8:
            return p & 1, p >> 1, 0
        q = p - 8
        return (q // 3) & 1, 3 - q // 6, (1, 3, 2)[q % 3]

    def group_target(p):
        core, y, z = distance(p)
        return ((half + core) & 1) * SLABS + (((slab >> 2) + y) & 3) * 4 + ((slab + z) & 3)

    def group_source(p):
        q = p - 8
        third = lax.rem(q, 3)
        near = p < 8
        core = jnp.where(near, p, q // 3) & 1
        y = jnp.where(near, p >> 1, 3 - q // 6)
        z = jnp.where(near, 0, jnp.where(third == 0, 1, jnp.where(third == 1, 3, 2)))
        row = ((slab >> 2) + 4 - y) & 3
        return ((half + core) & 1) * SLABS + row * 4 + ((slab + 4 - z) & 3)

    def group_peer(p):
        other = group_target(GROUP - 1 - p)
        return other, ring(other)

    def greet(peer, count):
        for p in range(count - 1):
            pl.semaphore_signal(
                pltpu.get_barrier_semaphore(), inc=1, device_id=peer(p)[1], device_id_type=MESH
            )

    load = pltpu.make_async_copy(
        sino.at[:, :, pl.ds(FIRST_COL, COLS)], views, local_sem.at[0]
    )
    load.start()
    greet(group_peer, GROUP)
    greet(pair_peer, 2 * SUBS)
    load.wait()

    table = view_table(angles)
    lane, row = iota((8, 128), 1), iota((8, 128), 0)

    def pack(q, carry):
        at = pl.multiple_of(q * 16, 16)
        zero = views[0, pl.ds(at, 16), :].astype(F32)
        one = views[1, pl.ds(at, 16), :].astype(F32)
        for i in range(4):
            both = jnp.concatenate([zero[4 * i : 4 * i + 4], one[4 * i : 4 * i + 4]], axis=0)
            ends = every_lane(both[:, :128], 127), every_lane(both[:, 1152:], 0)
            line = jnp.where(lane == row + 8, ends[0], table)
            line = jnp.where(lane == row + 16, ends[1], line)
            send_extra[4 * q + i] = jnp.sum(line, axis=0, keepdims=True)
            send[4 * q + i] = jnp.concatenate([both[:, 128:640], both[:, 640:1152]], axis=0).astype(
                BF16
            )
        return carry

    lax.fori_loop(0, GROUP // 4, pack, 0)
    recv[me] = send[me]
    recv_extra[me] = send_extra[me]
    own[...] = jnp.zeros_like(own)
    pl.semaphore_wait(pltpu.get_barrier_semaphore(), GROUP - 1 + 2 * SUBS - 1)

    def remote(src, dst, send_sem, recv_sem, target):
        return pltpu.make_async_remote_copy(
            src_ref=src,
            dst_ref=dst,
            send_sem=send_sem,
            recv_sem=recv_sem,
            device_id=target,
            device_id_type=MESH,
        )

    def data_copy(other, slot):
        return remote(
            send.at[other], recv.at[slot], data_send.at[other], data_recv.at[slot], ring(other)
        )

    def extra_copy(other, slot):
        return remote(
            send_extra.at[other],
            recv_extra.at[slot],
            extra_send.at[other],
            extra_recv.at[slot],
            ring(other),
        )

    for p in range(1, GROUP):
        extra_copy(group_target(p), me).start()
        data_copy(group_target(p), me).start()

    first_cat[...] = build_first(w_first[...], b_first[...])
    second_cat[...], second_t[...] = build_second(w_second[...])

    def two_senders(p, carry):
        for q in range(2):
            other = group_source(2 * p + q)

            def arrived(other=other):
                extra_copy(other, other).wait_recv()
                data_copy(other, other).wait_recv()

            if q == 0:
                pl.when(p > 0)(arrived)
            else:
                arrived()
        for q in range(2):
            other = group_source(2 * p + q)
            add_sender(recv[other], recv_extra[other], windows.at[q], own)
        return carry

    lax.fori_loop(0, GROUP // 2, two_senders, 0)
    own[...] = own[...] * (math.pi / VPS)

    to_after = remote(
        own.at[2:4], field.at[0:2], halo_send.at[0], halo_recv.at[0], ring(lax.rem(me + 1, GROUP))
    )
    to_before = remote(
        own.at[0:2], field.at[6:8], halo_send.at[1], halo_recv.at[1], ring(lax.rem(me + GROUP - 1, GROUP))
    )

    def eighth(index):
        return pl.ds(pl.multiple_of(index * 128, 128), 128)

    def part_copy(p, arriving):
        other, target = sub_peer(p)
        slot = other if arriving else sub
        return remote(
            own.at[:, :, eighth(other)],
            eighths.at[slot],
            part_send.at[other],
            part_recv.at[slot],
            target,
        )

    def total_copy(p, arriving):
        other, target = sub_peer(p)
        slot = other if arriving else sub
        return remote(
            piece, totals.at[:, :, eighth(slot)], tot_send.at[other], tot_recv.at[slot], target
        )

    def slab_copy(p, arriving):
        other, target = slab_peer(p)
        slot = other if arriving else slab
        return remote(
            mine.at[0], part_slots.at[slot], slab_send.at[other], slab_recv.at[slot], target
        )

    def pair_copy(p, arriving):
        other, target = pair_peer(p)
        slot = other if arriving else pair
        return remote(
            mine.at[1], whole_slots.at[slot], pair_send.at[other], pair_recv.at[slot], target
        )

    def started(make, count):
        for p in range(count - 1):
            make(p, False).start()

    def finished(make, count):
        for p in range(count - 1):
            make(p, True).wait()

    started(part_copy, SUBS)
    to_after.start()
    to_before.start()
    eighths[sub] = own[:, :, eighth(sub)]
    taps[...] = jnp.zeros_like(taps)
    near_r[...] = jnp.zeros_like(near_r)
    acc_first[...] = jnp.zeros_like(acc_first)
    acc_second[...] = jnp.zeros_like(acc_second)
    ones = (iota((8, X), 0) == 0).astype(F32)

    def place(m, value):
        near_u[m] = jnp.concatenate([shifted(value, 1), value, shifted(value, -1)], axis=0)

    def forward(j, carry):
        patch = jnp.concatenate([near_u[j], near_u[j + 1], near_u[j + 2], ones], axis=0)
        high, low = split(patch)
        patch_u[j] = high
        pre = jnp.dot(
            first_cat[...], jnp.concatenate([high, high, low], axis=0), preferred_element_type=F32
        )
        outside = ((j == 0) & (me == 0)) | ((j == 5) & (me == GROUP - 1))
        hidden = jnp.maximum(pre, 0.0) * jnp.where(outside, 0.0, 1.0)
        high, low = split(hidden)
        hidden_all[j] = high
        main = jnp.dot(second_t[...], high, preferred_element_type=F32)
        rest = jnp.dot(second_t[0:PATCH], low, preferred_element_type=F32)
        added = main[:72] + (main[PATCH : PATCH + 72] + rest[:72])
        for shift_z in range(3):
            at = j - shift_z + 2
            taps[at] = taps[at] + added[24 * shift_z : 24 * shift_z + 24]
        return carry

    for i in range(DEPTH):
        place(i + 2, own[i])
    lax.fori_loop(2, 4, forward, 0)
    gather_first[...], gather_second[...] = build_gather()
    finished(part_copy, SUBS)
    total = eighths[0]
    for s in range(1, SUBS):
        total = total + eighths[s]
    piece[...] = total
    totals[:, :, eighth(sub)] = total
    started(total_copy, SUBS)
    to_after.wait()
    to_before.wait()
    for m in range(2):
        place(m, jnp.where(me > 0, field[m], 0.0))
        place(m + 6, jnp.where(me < GROUP - 1, field[m + 6], 0.0))
    lax.fori_loop(0, 2, forward, 0)
    lax.fori_loop(4, 6, forward, 0)
    finished(total_copy, SUBS)

    sum_square = jnp.zeros((8, X), F32)
    sum_resid = jnp.zeros((8, X), F32)
    for i in range(DEPTH):
        value = own[i]
        conv = shifted(taps[i + 2, 0:8], 1) + taps[i + 2, 8:16] + shifted(taps[i + 2, 16:24], -1)
        pred = value + conv + b_second[0]
        target = (totals[i] - value) / (SUBS - 1)
        pred_out[i] = pred
        target_out[i] = target
        diff = pred - target
        resid = (2.0 * diff) / CELLS
        sum_square = sum_square + diff * diff
        sum_resid = sum_resid + resid
        near_r[i + 2] = jnp.concatenate([shifted(resid, -1), resid, shifted(resid, 1)], axis=0)

    nothing = jnp.zeros((8, X), F32)

    def backward(j, carry):
        patch = jnp.concatenate([near_r[j + 2], near_r[j + 1], near_r[j], nothing], axis=0)
        high, low = split(patch)
        grad = jnp.dot(
            second_cat[...], jnp.concatenate([high, high, low], axis=0), preferred_element_type=F32
        )
        hidden = hidden_all[j]
        acc_second[:, :PATCH] += dot_nt(hidden, high)
        grad = jnp.where(hidden.astype(F32) > 0.0, grad, 0.0).astype(BF16)
        acc_first[:, :PATCH] += dot_nt(grad, patch_u[j])
        return carry

    lax.fori_loop(0, 6, backward, 0, unroll=3)

    packed = gathered(acc_first[...], gather_first[...])
    packed = packed + gathered(acc_second[...], gather_second[...])
    packed = packed[:16] + pltpu.roll(packed[16:], 64, 1)
    row, lane = iota((16, 128), 0), iota((16, 128), 1)
    packed = packed + jnp.where((row == 0) & (lane == 60), jnp.sum(sum_square) / CELLS, 0.0)
    packed = packed + jnp.where((row == 0) & (lane == 61), jnp.sum(sum_resid), 0.0)

    mine[1] = packed
    whole_slots[pair] = packed
    started(pair_copy, 2 * SUBS)
    finished(pair_copy, 2 * SUBS)
    packed = whole_slots[0]
    for s in range(1, 16):
        packed = packed + whole_slots[s]
    mine[0] = packed
    part_slots[slab] = packed
    started(slab_copy, SLABS)
    finished(slab_copy, SLABS)
    packed = part_slots[0]
    for s in range(1, 16):
        packed = packed + part_slots[s]
    grads_out[...] = packed

    def sent(p, carry):
        other = lax.rem(me + p, GROUP)
        extra_copy(other, me).wait_send()
        data_copy(other, me).wait_send()
        return carry

    lax.fori_loop(1, GROUP, sent, 0)


def finish_kernel(pred, target, packed, pred_out, target_out, loss, g_w1, g_b1, g_w2, g_b2, sems):
    copies = [
        pltpu.make_async_copy(pred, pred_out, sems.at[0]),
        pltpu.make_async_copy(target, target_out, sems.at[1]),
    ]
    for copy in copies:
        copy.start()
    value = packed[...]
    both = jnp.concatenate([value, pltpu.roll(value, 64, 1)], axis=0)
    g_w1[...] = both[:, :27]
    g_w2[...] = both[:, 32:59]
    row, lane = iota((CH, 128), 0), iota((CH, 128), 1)
    column = jnp.sum(jnp.where(lane == 27, both, 0.0), axis=1, keepdims=True)
    g_b1[...] = jnp.sum(jnp.where(lane == row, column, 0.0), axis=0, keepdims=True)[:, :CH]
    loss[...] = value[0:1, 60:61]
    g_b2[...] = value[0:1, 61:62]
    for copy in copies:
        copy.wait()


VMEM = pl.BlockSpec(memory_space=pltpu.VMEM)
SMEM = pl.BlockSpec(memory_space=pltpu.SMEM)
ANY = pl.BlockSpec(memory_space=pl.ANY)
HBM = pl.BlockSpec(memory_space=pltpu.HBM)


def shape(dims, dtype=F32):
    return jax.ShapeDtypeStruct(dims, dtype)


def body(sinogram, angles, w_first, b_first, w_second, b_second):
    dma = pltpu.SemaphoreType.DMA
    vmem = pltpu.VMEM
    pred, target, grads = pl.pallas_call(
        step_kernel,
        name="train_step",
        out_shape=(shape((DEPTH, Y, X)), shape((DEPTH, Y, X)), shape((16, 128))),
        in_specs=[HBM, SMEM] + [VMEM] * 3 + [SMEM],
        out_specs=[VMEM] * 3,
        scratch_shapes=[
            vmem((2, 128, COLS), BF16),
            vmem((GROUP, 16, X // 2), BF16),
            vmem((GROUP, 16, X // 2), BF16),
            vmem((GROUP, 1, 128), F32),
            vmem((GROUP, 1, 128), F32),
            vmem((2, X // 128, 8, 384), F32),
            vmem((DEPTH, Y, X), F32),
            vmem((256, 3 * PATCH), BF16),
            vmem((256, 3 * PATCH), BF16),
            vmem((2 * PATCH, 256), BF16),
            vmem((1024, 128), BF16),
            vmem((1024, 128), BF16),
            vmem((8, Y, X), F32),
            vmem((SUBS, DEPTH, Y, 128), F32),
            vmem((DEPTH, Y, 128), F32),
            vmem((DEPTH, Y, X), F32),
            vmem((8, 24, X), F32),
            vmem((6, PATCH, X), BF16),
            vmem((6, 256, X), BF16),
            vmem((8, 24, X), F32),
            vmem((8, 24, X), F32),
            vmem((256, 128), F32),
            vmem((256, 128), F32),
            vmem((16, 16, 128), F32),
            vmem((16, 16, 128), F32),
            vmem((2, 16, 128), F32),
            dma((1,)),
            dma((GROUP,)),
            dma((GROUP,)),
            dma((GROUP,)),
            dma((GROUP,)),
            dma((2,)),
            dma((2,)),
        ]
        + [dma((SUBS,))] * 4
        + [dma((16,))] * 4,
        compiler_params=pltpu.CompilerParams(
            collective_id=0, has_side_effects=True, vmem_limit_bytes=62 << 20
        ),
    )(sinogram, angles, w_first, b_first[None], w_second, b_second)
    pred, target, loss, g_w1, g_b1, g_w2, g_b2 = pl.pallas_call(
        finish_kernel,
        name="finish",
        out_shape=(
            shape((1, DEPTH, Y, X)),
            shape((1, DEPTH, Y, X)),
            shape((1, 1)),
            shape((CH, 27)),
            shape((1, CH)),
            shape((CH, 27)),
            shape((1, 1)),
        ),
        in_specs=[VMEM] * 3,
        out_specs=[ANY] * 2 + [VMEM] * 5,
        scratch_shapes=[dma((2,))],
        compiler_params=pltpu.CompilerParams(vmem_limit_bytes=62 << 20),
    )(pred[None], target[None], grads)
    return pred, target, loss.reshape(()), g_w1, g_b1.reshape(CH), g_w2, g_b2.reshape(1)


def solution(mesh):
    finer = Mesh(mesh.devices.reshape(SUBS, 2, SLABS), ("sub", "half", "slab"))
    every = ("sub", "half", "slab")
    return jax.shard_map(
        body,
        mesh=finer,
        in_specs=(P(every, None, None), P(every), P(), P(), P(), P()),
        out_specs=(
            P(("sub", "half"), "slab", None, None),
            P(("sub", "half"), "slab", None, None),
            P(),
            P(),
            P(),
            P(),
            P(),
        ),
        check_vma=False,
    )
```

```python
import math

import jax
import jax.numpy as jnp
from jax import lax
from jax.experimental import pallas as pl
from jax.experimental.pallas import tpu as pltpu
from jax.sharding import Mesh
from jax.sharding import PartitionSpec as P

DET = 2048
X = 1024
Y = 8
CH = 32
DEPTH = 4
SUBS = 8
SLABS = 16
GROUP = 2 * SLABS
VPS = 64
FIRST_COL = 384
COLS = 1280
PATCH = 80
CELLS = float(SUBS * 128 * Y * X)
MESH = pl.DeviceIdType.MESH
F32 = jnp.float32
BF16 = jnp.bfloat16

GATHER = lax.GatherDimensionNumbers(
    offset_dims=(),
    collapsed_slice_dims=(1,),
    start_index_map=(1,),
    operand_batching_dims=(0,),
    start_indices_batching_dims=(0,),
)


def iota(shape, dim):
    return lax.broadcasted_iota(jnp.int32, shape, dim)


def exact_dot(a, b):
    return jnp.dot(a, b, precision=lax.Precision.HIGHEST, preferred_element_type=F32)


def dot_nt(a, b, precision=None):
    return lax.dot_general(
        a, b, (((1,), (1,)), ((), ())), precision=precision, preferred_element_type=F32
    )


def split(value):
    high = value.astype(BF16)
    return high, (value - high.astype(F32)).astype(BF16)


def tap_of(block, shift_y):
    shift_z = (block >= 3).astype(jnp.int32) + (block >= 6).astype(jnp.int32)
    return 6 * shift_z + block + 3 * shift_y


def build_first(w_first, b_first):
    pick = (iota((256, CH), 0) & (CH - 1) == iota((256, CH), 1)).astype(F32)
    rows = exact_dot(pick, w_first)
    bias = jnp.sum(pick * b_first, axis=1, keepdims=True)
    row, col = iota((256, PATCH), 0), iota((256, PATCH), 1)
    out = jnp.where(col == 72, bias, 0.0)
    tap, at = iota((27, PATCH), 0), iota((27, PATCH), 1)
    for shift_y in range(3):
        expand = ((tap == tap_of(at >> 3, shift_y)) & (at < 72)).astype(F32)
        near = (col & 7) - (row >> 5) == shift_y - 1
        out = out + jnp.where(near & (col < 72), exact_dot(rows, expand), 0.0)
    high, low = split(out)
    return jnp.concatenate([high, low, high], axis=1)


def build_second(w_second):
    pick = (iota((256, CH), 0) & (CH - 1) == iota((256, CH), 1)).astype(F32)
    rows = exact_dot(pick, w_second)
    row, col = iota((256, PATCH), 0), iota((256, PATCH), 1)
    pick_t = (iota((CH, 256), 1) & (CH - 1) == iota((CH, 256), 0)).astype(F32)
    row_t, col_t = iota((PATCH, 256), 0), iota((PATCH, 256), 1)
    out = jnp.zeros((256, PATCH), F32)
    out_t = jnp.zeros((PATCH, 256), F32)
    tap, at = iota((27, PATCH), 0), iota((27, PATCH), 1)
    tap_t, at_t = iota((PATCH, 27), 1), iota((PATCH, 27), 0)
    for shift_y in range(3):
        expand = ((tap == tap_of(at >> 3, shift_y)) & (at < 72)).astype(F32)
        near = (row >> 5) - (col & 7) == shift_y - 1
        out = out + jnp.where(near & (col < 72), exact_dot(rows, expand), 0.0)
        expand_t = ((tap_t == tap_of(at_t >> 3, shift_y)) & (at_t < 72)).astype(F32)
        taps_t = dot_nt(expand_t, w_second, lax.Precision.HIGHEST)
        near_t = (col_t >> 5) - (row_t & 7) == shift_y - 1
        out_t = out_t + jnp.where(near_t & (row_t < 72), exact_dot(taps_t, pick_t), 0.0)
    high, low = split(out)
    return jnp.concatenate([high, low, high], axis=1), jnp.concatenate(split(out_t), axis=0)


def build_gather():
    row, lane = iota((1024, 128), 0), iota((1024, 128), 1)
    y, col = row >> 7, row & 127
    block, near = col >> 3, col & 7
    shift = near - y + 1
    inside = (col < 72) & (shift >= 0) & (shift <= 2)
    first = (inside & (lane == tap_of(block, shift))) | ((col == 72) & (lane == 27))
    shift = y - near + 1
    inside = (col < 72) & (shift >= 0) & (shift <= 2)
    second = inside & (lane == tap_of(block, shift) + 32)
    return first.astype(F32).astype(BF16), second.astype(F32).astype(BF16)


def gathered(sums, gather):
    wide = jnp.concatenate([sums[CH * y : CH * y + CH] for y in range(Y)], axis=1)
    high, rest = wide.astype(BF16), wide
    rest = wide - high.astype(F32)
    middle, low = split(rest)
    out = jnp.dot(
        jnp.concatenate([high, middle, low], axis=0), gather, preferred_element_type=F32
    )
    return out[:CH] + (out[CH : 2 * CH] + out[2 * CH :])


def shifted(value, by):
    lane = iota(value.shape, 1)
    if by == 1:
        return jnp.where(lane == 0, 0.0, pltpu.roll(value, 1, 1))
    return jnp.where(lane == X - 1, 0.0, pltpu.roll(value, X - 1, 1))


def take(source, index):
    return lax.gather(
        source, index[..., None], GATHER, (1, 1), mode=lax.GatherScatterMode.PROMISE_IN_BOUNDS
    )


def view_table(angles):
    lane, row = iota((8, 128), 1), iota((8, 128), 0)
    angle = jnp.where(lane < 2, angles[0], angles[1])
    value = jnp.where(lane & 1 == 0, jnp.cos(angle), jnp.sin(angle))
    return jnp.where((row == 0) & (lane < 4), value, 0.0)


def every_lane(source, index):
    return take(source, jnp.full((8, 128), index, jnp.int32))


def window_range(part_x):
    ends = (abs(128 * part_x - 511.5), abs(128 * part_x - 384.5))
    middle = (DET - 1) / 2.0
    first = (math.floor(middle - max(ends) - 4.0) - FIRST_COL) // 64
    last = (math.floor(middle + min(ends) + 0.5) - FIRST_COL) // 64
    return first, last


def add_sender(block, extra, windows, out):
    value = block.astype(F32)
    tables = jnp.broadcast_to(extra, (8, 128))
    ends = [take(tables, iota((8, 128), 0) + at) for at in (8, 16)]
    row = jnp.concatenate([ends[0], value[:8], value[8:], ends[1]], axis=1)
    moved = pltpu.roll(row, COLS - 64, 1)
    views = [every_lane(tables, i) for i in range(4)]
    row_index = iota((8, 128), 0)
    row_pos = row_index.astype(F32) - (Y - 1) / 2.0
    lane = iota((8, 128), 1).astype(F32)

    def piece(k):
        source = moved if k & 1 else row
        return source[:, (k >> 1) * 128 : (k >> 1) * 128 + 128]

    lowest = []
    for part_x in range(X // 128):
        begin = 128.0 * part_x - (X - 1) / 2.0
        both = []
        for v in range(2):
            cosine, sine = views[2 * v], views[2 * v + 1]
            least = jnp.minimum(begin * cosine, (begin + 127.0) * cosine)
            both.append(jnp.floor((least - 3.5 * jnp.abs(sine)) + (DET - 1) / 2.0))
        lowest.append(both)
        offset = jnp.where(row_index < 4, both[0], both[1]) - float(FIRST_COL)
        step = jnp.floor(offset * (1.0 / 64.0))
        first, last = window_range(part_x)
        near, far = piece(first), piece(first + 2)
        for k in range(first + 1, last + 1):
            reached = step >= float(k)
            near = jnp.where(reached, piece(k), near)
            far = jnp.where(reached, piece(k + 2), far)
        moved_by = (offset - 64.0 * step).astype(jnp.int32)
        place = moved_by + iota((8, 128), 1)
        at = place & 127
        window = [
            jnp.where(place < 128, take(near, at), take(far, at)),
            take(far, moved_by),
            take(far, moved_by + 1),
        ]
        windows[part_x] = jnp.concatenate(window, axis=1)
    for part_x in range(X // 128):
        here = slice(part_x * 128, (part_x + 1) * 128)
        total = [out[z, :, here] for z in range(DEPTH)]
        for v in range(2):
            cosine, sine = views[2 * v], views[2 * v + 1]
            pos = (
                (lane + (128.0 * part_x - (X - 1) / 2.0)) * cosine + row_pos * sine
            ) + (DET - 1) / 2.0
            lower = jnp.floor(pos)
            part = pos - lower
            w_high = part.astype(BF16).astype(F32)
            w_low = (1.0 - part).astype(BF16).astype(F32)
            index = (lower - lowest[part_x][v]).astype(jnp.int32)
            index = jnp.concatenate([index, index], axis=0)
            at_low = (index & 127).astype(jnp.int16)
            at_high = ((index + 1) & 127).astype(jnp.int16)
            whole = index.astype(jnp.int16)
            in_low = whole < jnp.int16(128)
            in_high = whole < jnp.int16(127)
            for pair in range(2):

                def source(offset):
                    first_row = v * 4 + 2 * pair
                    parts = [
                        jnp.broadcast_to(
                            windows[part_x, pl.ds(first_row + q, 1), pl.ds(offset, 128)], (8, 128)
                        )
                        for q in range(2)
                    ]
                    return jnp.concatenate(parts, axis=0).astype(BF16)

                near, next_one, after = source(0), source(128), source(256)
                low = jnp.where(in_low, take(near, at_low), next_one).astype(F32)
                high = jnp.where(in_low, next_one, after)
                high = jnp.where(in_high, take(near, at_high), high).astype(F32)
                for q in range(2):
                    z = 2 * pair + q
                    half = slice(8 * q, 8 * q + 8)
                    total[z] = total[z] + (w_low * low[half] + w_high * high[half])
        for z in range(DEPTH):
            out[z, :, here] = total[z]


def step_kernel(
    sino,
    angles,
    w_first,
    b_first,
    w_second,
    b_second,
    pred_out,
    target_out,
    grads_out,
    views,
    send,
    recv,
    send_extra,
    recv_extra,
    windows,
    own,
    first_cat,
    second_cat,
    second_t,
    gather_first,
    gather_second,
    field,
    eighths,
    piece,
    totals,
    near_u,
    patch_u,
    hidden_all,
    taps,
    near_r,
    acc_first,
    acc_second,
    part_slots,
    whole_slots,
    mine,
    local_sem,
    data_send,
    data_recv,
    extra_send,
    extra_recv,
    halo_send,
    halo_recv,
    part_send,
    part_recv,
    tot_send,
    tot_recv,
    slab_send,
    slab_recv,
    pair_send,
    pair_recv,
):
    sub, half, slab = lax.axis_index("sub"), lax.axis_index("half"), lax.axis_index("slab")
    me = half * SLABS + slab
    pair = sub * 2 + half

    def ring(other):
        return (sub, other >> 4, other & 15)

    far_first = (2, 1, 3, 0)

    def slab_peer(p):
        y = ((slab >> 2) + far_first[p >> 2]) & 3
        other = y * 4 + ((slab + far_first[p & 3]) & 3)
        return other, (sub, half, other)

    def sub_at(p):
        x = ((sub >> 1) + far_first[p >> 1]) & 3
        return x * 2 + ((sub + 1 + p) & 1)

    def pair_peer(p):
        other_sub, other_half = sub_at(p >> 1), (half + 1 + p) & 1
        return other_sub * 2 + other_half, (other_sub, other_half, slab)

    def sub_peer(p):
        other = sub_at(p)
        return other, (other, half, slab)

    def distance(p):
        if p < 8:
            return p & 1, p >> 1, 0
        q = p - 8
        return (q // 3) & 1, 3 - q // 6, (1, 3, 2)[q % 3]

    def group_target(p):
        core, y, z = distance(p)
        return ((half + core) & 1) * SLABS + (((slab >> 2) + y) & 3) * 4 + ((slab + z) & 3)

    def group_source(p):
        q = p - 8
        third = lax.rem(q, 3)
        near = p < 8
        core = jnp.where(near, p, q // 3) & 1
        y = jnp.where(near, p >> 1, 3 - q // 6)
        z = jnp.where(near, 0, jnp.where(third == 0, 1, jnp.where(third == 1, 3, 2)))
        row = ((slab >> 2) + 4 - y) & 3
        return ((half + core) & 1) * SLABS + row * 4 + ((slab + 4 - z) & 3)

    def group_peer(p):
        other = group_target(GROUP - 1 - p)
        return other, ring(other)

    def greet(peer, count):
        for p in range(count - 1):
            pl.semaphore_signal(
                pltpu.get_barrier_semaphore(), inc=1, device_id=peer(p)[1], device_id_type=MESH
            )

    load = pltpu.make_async_copy(
        sino.at[:, :, pl.ds(FIRST_COL, COLS)], views, local_sem.at[0]
    )
    load.start()
    greet(group_peer, GROUP)
    greet(pair_peer, 2 * SUBS)
    load.wait()

    table = view_table(angles)
    lane, row = iota((8, 128), 1), iota((8, 128), 0)

    def pack(q, carry):
        at = pl.multiple_of(q * 16, 16)
        zero = views[0, pl.ds(at, 16), :].astype(F32)
        one = views[1, pl.ds(at, 16), :].astype(F32)
        for i in range(4):
            both = jnp.concatenate([zero[4 * i : 4 * i + 4], one[4 * i : 4 * i + 4]], axis=0)
            ends = every_lane(both[:, :128], 127), every_lane(both[:, 1152:], 0)
            line = jnp.where(lane == row + 8, ends[0], table)
            line = jnp.where(lane == row + 16, ends[1], line)
            send_extra[4 * q + i] = jnp.sum(line, axis=0, keepdims=True)
            send[4 * q + i] = jnp.concatenate([both[:, 128:640], both[:, 640:1152]], axis=0).astype(
                BF16
            )
        return carry

    lax.fori_loop(0, GROUP // 4, pack, 0)
    recv[me] = send[me]
    recv_extra[me] = send_extra[me]
    own[...] = jnp.zeros_like(own)
    pl.semaphore_wait(pltpu.get_barrier_semaphore(), GROUP - 1 + 2 * SUBS - 1)

    def remote(src, dst, send_sem, recv_sem, target):
        return pltpu.make_async_remote_copy(
            src_ref=src,
            dst_ref=dst,
            send_sem=send_sem,
            recv_sem=recv_sem,
            device_id=target,
            device_id_type=MESH,
        )

    def data_copy(other, slot):
        return remote(
            send.at[other], recv.at[slot], data_send.at[other], data_recv.at[slot], ring(other)
        )

    def extra_copy(other, slot):
        return remote(
            send_extra.at[other],
            recv_extra.at[slot],
            extra_send.at[other],
            extra_recv.at[slot],
            ring(other),
        )

    for p in range(1, GROUP):
        extra_copy(group_target(p), me).start()
        data_copy(group_target(p), me).start()

    first_cat[...] = build_first(w_first[...], b_first[...])
    second_cat[...], second_t[...] = build_second(w_second[...])

    def two_senders(p, carry):
        for q in range(2):
            other = group_source(2 * p + q)

            def arrived(other=other):
                extra_copy(other, other).wait_recv()
                data_copy(other, other).wait_recv()

            if q == 0:
                pl.when(p > 0)(arrived)
            else:
                arrived()
        for q in range(2):
            other = group_source(2 * p + q)
            add_sender(recv[other], recv_extra[other], windows.at[q], own)
        return carry

    lax.fori_loop(0, GROUP // 2, two_senders, 0)
    own[...] = own[...] * (math.pi / VPS)

    to_after = remote(
        own.at[2:4], field.at[0:2], halo_send.at[0], halo_recv.at[0], ring(lax.rem(me + 1, GROUP))
    )
    to_before = remote(
        own.at[0:2], field.at[6:8], halo_send.at[1], halo_recv.at[1], ring(lax.rem(me + GROUP - 1, GROUP))
    )

    def eighth(index):
        return pl.ds(pl.multiple_of(index * 128, 128), 128)

    def part_copy(p, arriving):
        other, target = sub_peer(p)
        slot = other if arriving else sub
        return remote(
            own.at[:, :, eighth(other)],
            eighths.at[slot],
            part_send.at[other],
            part_recv.at[slot],
            target,
        )

    def total_copy(p, arriving):
        other, target = sub_peer(p)
        slot = other if arriving else sub
        return remote(
            piece, totals.at[:, :, eighth(slot)], tot_send.at[other], tot_recv.at[slot], target
        )

    def slab_copy(p, arriving):
        other, target = slab_peer(p)
        slot = other if arriving else slab
        return remote(
            mine.at[0], part_slots.at[slot], slab_send.at[other], slab_recv.at[slot], target
        )

    def pair_copy(p, arriving):
        other, target = pair_peer(p)
        slot = other if arriving else pair
        return remote(
            mine.at[1], whole_slots.at[slot], pair_send.at[other], pair_recv.at[slot], target
        )

    def started(make, count):
        for p in range(count - 1):
            make(p, False).start()

    def finished(make, count):
        for p in range(count - 1):
            make(p, True).wait()

    started(part_copy, SUBS)
    to_after.start()
    to_before.start()
    eighths[sub] = own[:, :, eighth(sub)]
    taps[...] = jnp.zeros_like(taps)
    near_r[...] = jnp.zeros_like(near_r)
    acc_first[...] = jnp.zeros_like(acc_first)
    acc_second[...] = jnp.zeros_like(acc_second)
    ones = (iota((8, X), 0) == 0).astype(F32)

    def place(m, value):
        near_u[m] = jnp.concatenate([shifted(value, 1), value, shifted(value, -1)], axis=0)

    def forward(j, carry):
        patch = jnp.concatenate([near_u[j], near_u[j + 1], near_u[j + 2], ones], axis=0)
        high, low = split(patch)
        patch_u[j] = high
        pre = jnp.dot(
            first_cat[...], jnp.concatenate([high, high, low], axis=0), preferred_element_type=F32
        )
        outside = ((j == 0) & (me == 0)) | ((j == 5) & (me == GROUP - 1))
        hidden = jnp.maximum(pre, 0.0) * jnp.where(outside, 0.0, 1.0)
        high, low = split(hidden)
        hidden_all[j] = high
        main = jnp.dot(second_t[...], high, preferred_element_type=F32)
        rest = jnp.dot(second_t[0:PATCH], low, preferred_element_type=F32)
        added = main[:72] + (main[PATCH : PATCH + 72] + rest[:72])
        for shift_z in range(3):
            at = j - shift_z + 2
            taps[at] = taps[at] + added[24 * shift_z : 24 * shift_z + 24]
        return carry

    for i in range(DEPTH):
        place(i + 2, own[i])
    lax.fori_loop(2, 4, forward, 0)
    gather_first[...], gather_second[...] = build_gather()
    finished(part_copy, SUBS)
    total = eighths[0]
    for s in range(1, SUBS):
        total = total + eighths[s]
    piece[...] = total
    totals[:, :, eighth(sub)] = total
    started(total_copy, SUBS)
    to_after.wait()
    to_before.wait()
    for m in range(2):
        place(m, jnp.where(me > 0, field[m], 0.0))
        place(m + 6, jnp.where(me < GROUP - 1, field[m + 6], 0.0))
    lax.fori_loop(0, 2, forward, 0)
    lax.fori_loop(4, 6, forward, 0)
    finished(total_copy, SUBS)

    sum_square = jnp.zeros((8, X), F32)
    sum_resid = jnp.zeros((8, X), F32)
    for i in range(DEPTH):
        value = own[i]
        conv = shifted(taps[i + 2, 0:8], 1) + taps[i + 2, 8:16] + shifted(taps[i + 2, 16:24], -1)
        pred = value + conv + b_second[0]
        target = (totals[i] - value) / (SUBS - 1)
        pred_out[i] = pred
        target_out[i] = target
        diff = pred - target
        resid = (2.0 * diff) / CELLS
        sum_square = sum_square + diff * diff
        sum_resid = sum_resid + resid
        near_r[i + 2] = jnp.concatenate([shifted(resid, -1), resid, shifted(resid, 1)], axis=0)

    nothing = jnp.zeros((8, X), F32)

    def backward(j, carry):
        patch = jnp.concatenate([near_r[j + 2], near_r[j + 1], near_r[j], nothing], axis=0)
        high, low = split(patch)
        grad = jnp.dot(
            second_cat[...], jnp.concatenate([high, high, low], axis=0), preferred_element_type=F32
        )
        hidden = hidden_all[j]
        acc_second[:, :PATCH] += dot_nt(hidden, high)
        grad = jnp.where(hidden.astype(F32) > 0.0, grad, 0.0).astype(BF16)
        acc_first[:, :PATCH] += dot_nt(grad, patch_u[j])
        return carry

    lax.fori_loop(0, 6, backward, 0, unroll=3)

    packed = gathered(acc_first[...], gather_first[...])
    packed = packed + gathered(acc_second[...], gather_second[...])
    packed = packed[:16] + pltpu.roll(packed[16:], 64, 1)
    row, lane = iota((16, 128), 0), iota((16, 128), 1)
    packed = packed + jnp.where((row == 0) & (lane == 60), jnp.sum(sum_square) / CELLS, 0.0)
    packed = packed + jnp.where((row == 0) & (lane == 61), jnp.sum(sum_resid), 0.0)

    mine[1] = packed
    whole_slots[pair] = packed
    started(pair_copy, 2 * SUBS)
    finished(pair_copy, 2 * SUBS)
    packed = jnp.sum(whole_slots[...], axis=0)
    mine[0] = packed
    part_slots[slab] = packed
    started(slab_copy, SLABS)
    finished(slab_copy, SLABS)
    packed = jnp.sum(part_slots[...], axis=0)
    grads_out[...] = packed

    def sent(p, carry):
        other = lax.rem(me + p, GROUP)
        extra_copy(other, me).wait_send()
        data_copy(other, me).wait_send()
        return carry

    lax.fori_loop(1, GROUP, sent, 0)


def finish_kernel(pred, target, packed, pred_out, target_out, loss, g_w1, g_b1, g_w2, g_b2, sems):
    copies = [
        pltpu.make_async_copy(pred, pred_out, sems.at[0]),
        pltpu.make_async_copy(target, target_out, sems.at[1]),
    ]
    for copy in copies:
        copy.start()
    value = packed[...]
    both = jnp.concatenate([value, pltpu.roll(value, 64, 1)], axis=0)
    g_w1[...] = both[:, :27]
    g_w2[...] = both[:, 32:59]
    row, lane = iota((CH, 128), 0), iota((CH, 128), 1)
    column = jnp.sum(jnp.where(lane == 27, both, 0.0), axis=1, keepdims=True)
    g_b1[...] = jnp.sum(jnp.where(lane == row, column, 0.0), axis=0, keepdims=True)[:, :CH]
    loss[...] = value[0:1, 60:61]
    g_b2[...] = value[0:1, 61:62]
    for copy in copies:
        copy.wait()


VMEM = pl.BlockSpec(memory_space=pltpu.VMEM)
SMEM = pl.BlockSpec(memory_space=pltpu.SMEM)
ANY = pl.BlockSpec(memory_space=pl.ANY)
HBM = pl.BlockSpec(memory_space=pltpu.HBM)


def shape(dims, dtype=F32):
    return jax.ShapeDtypeStruct(dims, dtype)


def body(sinogram, angles, w_first, b_first, w_second, b_second):
    dma = pltpu.SemaphoreType.DMA
    vmem = pltpu.VMEM
    pred, target, grads = pl.pallas_call(
        step_kernel,
        name="train_step",
        out_shape=(shape((DEPTH, Y, X)), shape((DEPTH, Y, X)), shape((16, 128))),
        in_specs=[HBM, SMEM] + [VMEM] * 3 + [SMEM],
        out_specs=[VMEM] * 3,
        scratch_shapes=[
            vmem((2, 128, COLS), BF16),
            vmem((GROUP, 16, X // 2), BF16),
            vmem((GROUP, 16, X // 2), BF16),
            vmem((GROUP, 1, 128), F32),
            vmem((GROUP, 1, 128), F32),
            vmem((2, X // 128, 8, 384), F32),
            vmem((DEPTH, Y, X), F32),
            vmem((256, 3 * PATCH), BF16),
            vmem((256, 3 * PATCH), BF16),
            vmem((2 * PATCH, 256), BF16),
            vmem((1024, 128), BF16),
            vmem((1024, 128), BF16),
            vmem((8, Y, X), F32),
            vmem((SUBS, DEPTH, Y, 128), F32),
            vmem((DEPTH, Y, 128), F32),
            vmem((DEPTH, Y, X), F32),
            vmem((8, 24, X), F32),
            vmem((6, PATCH, X), BF16),
            vmem((6, 256, X), BF16),
            vmem((8, 24, X), F32),
            vmem((8, 24, X), F32),
            vmem((256, 128), F32),
            vmem((256, 128), F32),
            vmem((16, 16, 128), F32),
            vmem((16, 16, 128), F32),
            vmem((2, 16, 128), F32),
            dma((1,)),
            dma((GROUP,)),
            dma((GROUP,)),
            dma((GROUP,)),
            dma((GROUP,)),
            dma((2,)),
            dma((2,)),
        ]
        + [dma((SUBS,))] * 4
        + [dma((16,))] * 4,
        compiler_params=pltpu.CompilerParams(
            collective_id=0, has_side_effects=True, vmem_limit_bytes=62 << 20
        ),
    )(sinogram, angles, w_first, b_first[None], w_second, b_second)
    pred, target, loss, g_w1, g_b1, g_w2, g_b2 = pl.pallas_call(
        finish_kernel,
        name="finish",
        out_shape=(
            shape((1, DEPTH, Y, X)),
            shape((1, DEPTH, Y, X)),
            shape((1, 1)),
            shape((CH, 27)),
            shape((1, CH)),
            shape((CH, 27)),
            shape((1, 1)),
        ),
        in_specs=[VMEM] * 3,
        out_specs=[ANY] * 2 + [VMEM] * 5,
        scratch_shapes=[dma((2,))],
        compiler_params=pltpu.CompilerParams(vmem_limit_bytes=62 << 20),
    )(pred[None], target[None], grads)
    return pred, target, loss.reshape(()), g_w1, g_b1.reshape(CH), g_w2, g_b2.reshape(1)


def solution(mesh):
    finer = Mesh(mesh.devices.reshape(SUBS, 2, SLABS), ("sub", "half", "slab"))
    every = ("sub", "half", "slab")
    return jax.shard_map(
        body,
        mesh=finer,
        in_specs=(P(every, None, None), P(every), P(), P(), P(), P()),
        out_specs=(
            P(("sub", "half"), "slab", None, None),
            P(("sub", "half"), "slab", None, None),
            P(),
            P(),
            P(),
            P(),
            P(),
        ),
        check_vma=False,
    )
```
